256 devices in a mesh: band: 128 (over z, y, x_hi, core), col: 2 (over x_lo).
Axes of the slice: x: 4 (x_hi: 2, x_lo: 2; x = x_hi * 2 + x_lo), y: 4, z: 8, core: 2. Of those that a mesh axis runs over, the one named last changes fastest.
Arguments:
- image: bfloat16 [512, 128, 512], P('band'), may hold values from -60 to 60
- timestep: int32 [1], replicated, may hold values from 0 to 999
- class_label: int32 [1], replicated, may hold values from 0 to 999
- class_table: bfloat16 [1000, 256], replicated, may hold values from -6 to 6
- fine_modulation: bfloat16 [256, 512], replicated, may hold values from -0.1875 to 0.1875
- coarse_modulation: bfloat16 [256, 1024], P(None, 'col'), may hold values from -0.1875 to 0.1875
- fine_project: bfloat16 [512, 1536], P(None, 'col'), may hold values from -0.25 to 0.25
- fine_output: bfloat16 [512, 512], P('col'), may hold values from -0.25 to 0.25
- fine_scales: float32 [8], replicated, may hold values from 4 to 12
- merge_weight: bfloat16 [8192, 1024], P(None, 'col'), may hold values from -0.0625 to 0.0625
- coarse_project: bfloat16 [1024, 3072], P('col', 'band'), may hold values from -0.1875 to 0.1875
- coarse_scales: float32 [16], replicated, may hold values from 8 to 16
Outputs:
- fine_mixed: bfloat16 [512, 128, 512], P('band', None, 'col')
- coarse_values: bfloat16 [128, 32, 1024], P('band', None, 'col')
The draws below stay inside these ranges and needn't reach their ends.
All inputs are finite; a program needn't handle non-finite values.
Results may differ from the reference program's by a relative error of at most 0.04.
Values may be sent and summed in bfloat16 or wider, within the bound.
A program may use at most 64 MiB of HBM per device.

```python
import math
import jax
import jax.numpy as jnp
from jax import lax

D5 = 512
DC = 1024
HD = 64
MAPW = 256
CLASSES = 1000
KW = 7
MERGE = 4
C5 = 128
HF = 8
HC = 16
ROWS5 = 512


def draw_image(key, part):
    key = jax.random.fold_in(key, 17)
    first, second, third = jax.random.split(key, 3)
    token_scale = jnp.exp(jax.random.uniform(second, (ROWS5, C5, 1)) * math.log(10.0))
    feature_scale = jnp.exp(jax.random.uniform(third, (D5,)) * math.log(10.0))
    sample = jnp.clip(jax.random.normal(first, (ROWS5, C5, D5)), -6.0, 6.0)
    return (0.1 * sample * token_scale * feature_scale).astype(jnp.bfloat16)


def block_levels(key, shape, cuts, smallest, largest):
    factor_of = 1.0
    for axis_at, shards_of in cuts:
        steps = jax.random.uniform(jax.random.fold_in(jax.random.fold_in(key, 6), axis_at), (shards_of,), jnp.float32, smallest / len(cuts), largest / len(cuts))
        factor_of = factor_of * jnp.repeat(jnp.exp(steps), shape[axis_at] // shards_of).reshape((-1,) + (1,) * (len(shape) - 1 - axis_at))
    return factor_of


def centred(key, extent, deviation, reach, cuts=(), held_as=jnp.bfloat16):
    entries = deviation * jax.random.normal(key, extent, jnp.float32)
    if cuts:
        entries = entries * block_levels(key, extent, cuts, -0.22, 0.18)
    return jnp.clip(entries, -reach, reach).astype(held_as)


def setup_inputs(seed: int = 0) -> dict:
    key_of = jax.random.split(jax.random.key(seed), 13)
    return {
        "image": draw_image(jax.random.fold_in(key_of[12], 71), 0),
        "timestep": jax.random.randint(key_of[1], (1,), 0, 1000).astype(jnp.int32),
        "class_label": jax.random.randint(key_of[2], (1,), 0, CLASSES).astype(jnp.int32),
        "class_table": centred(key_of[3], (CLASSES, MAPW), 1.0, 6.0),
        "fine_modulation": centred(key_of[4], (MAPW, D5), (4 * MAPW) ** -0.5, 0.1875),
        "coarse_modulation": centred(key_of[5], (MAPW, DC), (4 * MAPW) ** -0.5, 0.1875, ((1, 2),)),
        "fine_project": centred(key_of[6], (D5, 3 * D5), D5 ** -0.5, 0.25, ((1, 2),)),
        "fine_output": centred(key_of[7], (D5, D5), D5 ** -0.5, 0.25, ((0, 2),)),
        "fine_scales": jnp.clip(jnp.exp(jax.random.uniform(key_of[8], (HF,), jnp.float32, math.log(4.0), math.log(12.0))), 4.0, 12.0),
        "merge_weight": centred(key_of[9], (MERGE * MERGE * D5, DC), (MERGE * MERGE * D5) ** -0.5, 0.0625, ((1, 2),)),
        "coarse_project": centred(key_of[10], (DC, 3 * DC), DC ** -0.5, 0.1875, ((0, 2), (1, 128))),
        "coarse_scales": jnp.clip(jnp.exp(jax.random.uniform(key_of[11], (HC,), jnp.float32, math.log(8.0), math.log(16.0))), 8.0, 16.0),
    }


EPSILON = 1e-06

def time_features(timestep, feature_count):
    half_width = feature_count // 2
    frequency = jnp.exp(-math.log(10000.0) * jnp.arange(half_width, dtype=jnp.float32) / half_width)
    angles = timestep.astype(jnp.float32) * frequency
    return jnp.concatenate([jnp.cos(angles), jnp.sin(angles)])

def unit_rows(values):
    scaled_rows = values * lax.rsqrt(lax.optimization_barrier(jnp.mean(values * values, axis=-1, keepdims=True)) + EPSILON)
    return (scaled_rows * (1.0 / math.sqrt(values.shape[-1]))).astype(jnp.bfloat16)

def reference(image, timestep, class_label, class_table, fine_modulation, coarse_modulation, fine_project, fine_output, fine_scales, merge_weight, coarse_project, coarse_scales):
    condition = class_table[class_label[0]].astype(jnp.float32) + time_features(timestep[0], MAPW)
    fine_gain = 1.0 + jnp.dot(condition, fine_modulation.astype(jnp.float32), precision=lax.Precision.HIGHEST)
    coarse_gain = 1.0 + jnp.dot(condition, coarse_modulation.astype(jnp.float32), precision=lax.Precision.HIGHEST)
    pixels = image.astype(jnp.float32)
    normed = (pixels * lax.rsqrt(lax.optimization_barrier(jnp.mean(pixels * pixels, axis=-1, keepdims=True)) + EPSILON) * fine_gain).astype(jnp.bfloat16)
    grid_height = ROWS5
    grid_width = C5
    project = jnp.dot(normed.reshape(-1, D5), fine_project, preferred_element_type=jnp.float32).astype(jnp.bfloat16)
    project = project.reshape(grid_height, grid_width, HF, 3, HD)
    queries = unit_rows(project[:, :, :, 0, :].astype(jnp.float32)).astype(jnp.float32)
    keys_all = unit_rows(project[:, :, :, 1, :].astype(jnp.float32))
    values_all = project[:, :, :, 2, :]
    radius = KW // 2
    padding = ((radius, radius), (radius, radius), (0, 0), (0, 0))
    keys_pad = jnp.pad(keys_all, padding)
    values_pad = jnp.pad(values_all, padding)
    row_ids = jnp.arange(grid_height, dtype=jnp.int32)[:, None]
    col_ids = jnp.arange(grid_width, dtype=jnp.int32)[None, :]
    numerator = jnp.zeros((grid_height, grid_width, HF, HD), jnp.float32)
    denominator = jnp.zeros((grid_height, grid_width, HF), jnp.float32)
    for row_off in range(-radius, radius + 1):
        for col_off in range(-radius, radius + 1):
            key_win = keys_pad[radius + row_off:radius + row_off + grid_height, radius + col_off:radius + col_off + grid_width].astype(jnp.float32)
            val_win = values_pad[radius + row_off:radius + row_off + grid_height, radius + col_off:radius + col_off + grid_width].astype(jnp.float32)
            inside = ((row_ids + row_off >= 0) & (row_ids + row_off < grid_height) & (col_ids + col_off >= 0) & (col_ids + col_off < grid_width)).astype(jnp.float32)
            logits = fine_scales * lax.optimization_barrier(jnp.sum(queries * key_win, axis=-1))
            weight = jnp.exp(logits) * inside[:, :, None]
            numerator = numerator + weight[:, :, :, None] * val_win
            denominator = denominator + weight
    attended = (numerator / denominator[:, :, :, None]).astype(jnp.bfloat16).reshape(-1, D5)
    fine_mixed = (pixels.reshape(-1, D5) + jnp.dot(attended, fine_output, preferred_element_type=jnp.float32)).astype(jnp.bfloat16)
    fine_mixed = fine_mixed.reshape(grid_height, grid_width, D5)
    coarse_rows = grid_height // MERGE
    coarse_cols = grid_width // MERGE
    patches = fine_mixed.reshape(coarse_rows, MERGE, coarse_cols, MERGE, D5).transpose(0, 2, 1, 3, 4).reshape(coarse_rows * coarse_cols, MERGE * MERGE * D5)
    merged = jnp.dot(patches, merge_weight, preferred_element_type=jnp.float32).astype(jnp.bfloat16)
    merged_wide = merged.astype(jnp.float32)
    factor = lax.rsqrt(lax.optimization_barrier(jnp.mean(merged_wide * merged_wide, axis=-1)) + EPSILON)
    scaled = (merged_wide * coarse_gain).astype(jnp.bfloat16)
    coarse_qkv = (factor[:, None] * jnp.dot(scaled, coarse_project, preferred_element_type=jnp.float32)).astype(jnp.bfloat16)
    coarse_qkv = coarse_qkv.reshape(coarse_rows * coarse_cols, HC, 3, HD).transpose(1, 0, 2, 3)

    def one_head(head_pack):
        head_qkv, head_scale = head_pack
        head_queries = unit_rows(head_qkv[:, 0, :].astype(jnp.float32))
        head_keys = unit_rows(head_qkv[:, 1, :].astype(jnp.float32))
        head_logits = head_scale * jnp.dot(head_queries, head_keys.T, preferred_element_type=jnp.float32)
        head_weights = jnp.exp(head_logits)
        head_numer = jnp.dot(head_weights.astype(jnp.bfloat16), head_qkv[:, 2, :], preferred_element_type=jnp.float32)
        head_denom = lax.optimization_barrier(jnp.sum(head_weights, axis=-1))
        return (head_numer / head_denom[:, None]).astype(jnp.bfloat16)
    per_head = lax.map(one_head, (coarse_qkv, coarse_scales))
    coarse_values = per_head.transpose(1, 0, 2).reshape(coarse_rows, coarse_cols, HC * HD)
    return (fine_mixed, coarse_values)
```

```python
import math

import jax
import jax.numpy as jnp
from jax import lax
from jax.experimental import pallas as pl
from jax.experimental.pallas import tpu as pltpu
from jax.sharding import PartitionSpec as P

EPSILON = 1e-06
LOG2E = math.log2(math.e)
BF = jnp.bfloat16
F32 = jnp.float32
MESH = pl.DeviceIdType.MESH
BANDS = 128


def dot(a, b):
    return jnp.dot(a, b, preferred_element_type=F32)


def dot_t(a, b):
    return lax.dot_general(a, b, (((1,), (1,)), ((), ())), preferred_element_type=F32)


def iota(shape, dim):
    return lax.broadcasted_iota(jnp.int32, shape, dim)


def kernel(
    timestep,
    label,
    fine_scales,
    coarse_scales,
    image,
    class_table,
    fine_modulation,
    coarse_modulation,
    fine_project,
    fine_output,
    merge_weight,
    coarse_project,
    fine_out,
    coarse_out,
    xb,
    table_v,
    fmod_v,
    cmod_v,
    fproj_v,
    wperm,
    fout_v,
    merge_v,
    cproj_v,
    qs,
    kb,
    vb,
    att_own,
    att_got,
    fine_v,
    macc,
    mg,
    gb,
    gain_v,
    wb,
    kvs,
    qsend,
    kvb,
    qb,
    num,
    den,
    ob,
    rb,
    cv_v,
    load_sem,
    merge_sem,
    halo_send,
    halo_recv,
    pair_send,
    pair_recv,
    att_send,
    att_recv,
    fine_sem,
    w_send,
    w_recv,
    g_send,
    g_recv,
    kv_send,
    kv_recv,
    q_send,
    q_recv,
    fw_send,
    fw_recv,
    r_send,
    r_recv,
):
    band = lax.axis_index("band")
    c = lax.axis_index("col")
    core = lax.rem(band, 2)
    xh = lax.rem(lax.div(band, 2), 2)
    y = lax.rem(lax.div(band, 4), 4)
    z = lax.div(band, 16)
    x = 2 * xh + c

    def dev(zz, yy, xx, kk):
        return (((zz * 4 + yy) * 2 + lax.div(xx, 2)) * 2 + kk, lax.rem(xx, 2))

    sibling = dev(z, y, x, 1 - core)
    partner = (band, 1 - c)
    slow = (lax.rem(band + BANDS - 1 + 2 * core, BANDS), 1 - c)

    def row_of(u):
        return u + (1 - core) * (3 - 2 * u)

    def load(src, dst, k):
        return pltpu.make_async_copy(src, dst, load_sem.at[k])

    loads = [
        load(fine_modulation, fmod_v, 4),
        load(class_table, table_v, 5),
        load(fine_project, fproj_v, 6),
        load(coarse_modulation, cmod_v, 7),
        load(coarse_project, cproj_v, 8),
        load(fine_output, fout_v.at[c], 9),
    ]
    rows = [load(image.at[row_of(u)], xb.at[3 + u], u) for u in range(4)]
    merges = [
        pltpu.make_async_copy(merge_weight.at[row_of(u)], merge_v.at[u], merge_sem.at[u])
        for u in range(4)
    ]
    for copy in loads[:3]:
        copy.start()
    for copy in rows:
        copy.start()
    for copy in loads[3:]:
        copy.start()

    barrier = pltpu.get_barrier_semaphore()

    def signal(device):
        pl.semaphore_signal(barrier, inc=1, device_id=device, device_id_type=MESH)

    signal(slow)
    signal(sibling)

    def signal_line(k, carry):
        signal(dev(lax.rem(z + lax.div(k, 4), 8), y, lax.rem(x + lax.rem(k, 4), 4), core))
        return carry

    def signal_plane(k, carry):
        signal(dev(z, lax.rem(y + lax.div(k, 4), 4), lax.rem(x + lax.rem(k, 4), 4), core))
        return carry

    lax.fori_loop(1, 32, signal_line, 0)
    lax.fori_loop(4, 16, signal_plane, 0)
    pl.semaphore_wait(barrier, 45)

    def remote(src, dst, send, recv, device):
        return pltpu.make_async_remote_copy(
            src_ref=src,
            dst_ref=dst,
            send_sem=send,
            recv_sem=recv,
            device_id=device,
            device_id_type=MESH,
        )

    slow_copies = [
        remote(
            image.at[row_of(3 - j)], xb.at[7 + j], halo_send.at[j], halo_recv.at[j], slow
        )
        for j in range(3)
    ]
    fast_copies = [
        remote(
            image.at[row_of(j)], xb.at[2 - j], halo_send.at[3 + j], halo_recv.at[3 + j], sibling
        )
        for j in range(3)
    ]
    for copy in slow_copies + fast_copies:
        copy.start()
    fout_copy = remote(fine_output, fout_v.at[c], pair_send.at[0], pair_recv.at[0], partner)
    fout_copy.start()
    for copy in merges:
        copy.start()

    loads[4].wait()
    eye = (iota((32, 24), 0) == iota((32, 24), 1)).astype(BF)
    wb[core, y, x] = dot_t(eye, cproj_v[...]).astype(BF)

    def w_line(k):
        return remote(
            wb.at[core, y, x],
            wb.at[core, y, x],
            w_send.at[k],
            w_recv.at[k],
            dev(z, y, lax.rem(x + k, 4), core),
        )

    def w_plane(k):
        return remote(
            wb.at[core, y],
            wb.at[core, y],
            w_send.at[3 + k],
            w_recv.at[3 + k],
            dev(z, lax.rem(y + k, 4), x, core),
        )

    w_core = remote(wb.at[core], wb.at[core], w_send.at[0], w_recv.at[0], sibling)
    for k in (1, 2, 3):
        w_line(k).start()

    lane = iota((8, 256), 1)
    freq = jnp.exp((-math.log(10000.0) / 128.0) * lax.rem(lane, 128).astype(F32))
    angle = timestep[0].astype(F32) * freq
    time = jnp.where(lane < 128, jnp.cos(angle), jnp.sin(angle))
    one_hot = (iota((8, 1000), 1) == label[0]).astype(F32).astype(BF)
    loads[1].wait()
    condition = dot(one_hot, table_v[...]) + time
    c_hi = condition.astype(BF)
    rest = condition - c_hi.astype(F32)
    c_mid = rest.astype(BF)
    c_lo = (rest - c_mid.astype(F32)).astype(BF)

    def gain_of(weights):
        return 1.0 + (dot(c_hi, weights) + (dot(c_mid, weights) + dot(c_lo, weights)))

    loads[0].wait()
    fine_gain = gain_of(fmod_v[...])[0:1, :]
    loads[3].wait()
    gain_v[c] = gain_of(cmod_v[...])
    gain_copy = remote(gain_v.at[c], gain_v.at[c], pair_send.at[1], pair_recv.at[1], partner)
    gain_copy.start()

    loads[2].wait()
    fp = fproj_v[...]
    for part in range(3):
        for h in range(4):
            wperm[:, 256 * part + 64 * h : 256 * part + 64 * h + 64] = fp[
                :, 192 * h + 64 * part : 192 * h + 64 * part + 64
            ]
    ones_block = (lax.div(iota((256, 256), 0), 64) == lax.div(iota((256, 256), 1), 64)).astype(
        F32
    ).astype(BF)
    lane_head = lax.div(iota((1, 256), 1), 64)
    q_scale = jnp.zeros((1, 256), F32)
    for h in range(4):
        q_scale = jnp.where(lane_head == h, fine_scales[4 * c + h] * (LOG2E / 8.0), q_scale)

    def unit_factor(u):
        sq = u * u
        hi = sq.astype(BF)
        lo = (sq - hi.astype(F32)).astype(BF)
        return lax.rsqrt((dot(hi, ones_block) + dot(lo, ones_block)) * (1.0 / 64.0) + EPSILON)

    def normed_of(pixels):
        wide = pixels.astype(F32)
        mean = jnp.mean(wide * wide, axis=-1, keepdims=True)
        return (wide * lax.rsqrt(mean + EPSILON) * fine_gain).astype(BF)

    def keys_values(normed):
        kv = dot(normed, wperm[:, 256:768]).astype(BF)
        key = kv[:, :256].astype(F32)
        return (key * unit_factor(key) * 0.125).astype(BF), kv[:, 256:]

    for copy in rows:
        copy.wait()
    normed = normed_of(xb[3:7].reshape(512, 512))
    key, value = keys_values(normed)
    kb[3:7] = key.reshape(4, 128, 256)
    vb[3:7] = value.reshape(4, 128, 256)
    query = dot(normed, wperm[:, 0:256]).astype(BF).astype(F32)
    query = query * unit_factor(query) * q_scale
    for h in range(4):
        qs[:, 128 * h : 128 * h + 128, :] = (
            jnp.where(lane_head == h, query, 0.0).astype(BF).reshape(4, 128, 256)
        )
    for copy in fast_copies:
        copy.wait_recv()
    key, value = keys_values(normed_of(xb[0:3].reshape(384, 512)))
    kb[0:3] = key.reshape(3, 128, 256)
    vb[0:3] = value.reshape(3, 128, 256)

    distance = iota((128, 128), 0) - iota((128, 128), 1)
    far = jnp.where((distance <= 3) & (distance >= -3), 0.0, -1e30)
    macc[...] = jnp.zeros_like(macc)
    perm = (iota((128, 128), 1) == 4 * lax.rem(iota((128, 128), 0), 32) + lax.div(iota((128, 128), 0), 32)).astype(F32).astype(BF)

    def att_copy(r):
        return remote(att_own.at[r], att_got.at[r], att_send.at[r], att_recv.at[r], partner)

    def fine_copy(r):
        return pltpu.make_async_copy(fine_v.at[r], fine_out.at[row_of(r)], fine_sem.at[r])

    def attend_row(r):
        keys = kb[pl.ds(r, 7)].reshape(896, 256)
        values = vb[pl.ds(r, 7)].reshape(896, 256)
        bias = []
        for d in range(7):
            row = 4 * band + row_of(r + d - 3)
            outside = jnp.where((row < 0) | (row >= 4 * BANDS), -1e30, 0.0)
            bias.append(far + outside)
        bias = jnp.concatenate(bias, axis=1)
        logits = dot_t(qs[r], keys).reshape(4, 128, 896) + bias[None]
        weight = jnp.exp2(logits)
        total = jnp.sum(weight, axis=-1, keepdims=True)
        out = dot(weight.astype(BF).reshape(512, 896), values).reshape(4, 128, 256) * (1.0 / total)
        mixed = jnp.zeros((128, 256), F32)
        for h in range(4):
            mixed = jnp.where(lane_head == h, out[h], mixed)
        att_own[r] = mixed.astype(BF)
        att_copy(r).start()

    def mix_row(r):
        att_copy(r).wait_recv()
        merge_copy = pltpu.make_async_copy(
            merge_weight.at[row_of(r)], merge_v.at[r], merge_sem.at[r]
        )
        merge_copy.wait()
        full = (
            xb[3 + r].astype(F32) + dot(att_own[r], fout_v[c]) + dot(att_got[r], fout_v[1 - c])
        )
        fine_v[r] = jnp.where(c == 0, full[:, :256], full[:, 256:]).astype(BF)
        fine_copy(r).start()
        patches = dot(perm, full.astype(BF)).astype(BF)
        part = macc[...]
        for p in range(4):
            part = part + dot(patches[32 * p : 32 * p + 32], merge_v[r, 512 * p : 512 * p + 512, :])
        macc[...] = part

    def row_step(r, carry):
        @pl.when((r >= 1) & (r < 4))
        def _():
            slow_copy = remote(
                image.at[row_of(4 - r)],
                xb.at[6 + r],
                halo_send.at[r - 1],
                halo_recv.at[r - 1],
                slow,
            )
            slow_copy.wait_recv()
            key, value = keys_values(normed_of(xb[6 + r]))
            kb[6 + r] = key
            vb[6 + r] = value

        @pl.when(r < 4)
        def _():
            attend_row(r)

        @pl.when(r == 1)
        def _():
            for k in (1, 2, 3):
                w_line(k).wait_recv()
            for k in (1, 2, 3):
                w_plane(k).start()

        @pl.when(r == 3)
        def _():
            for k in (1, 2, 3):
                w_plane(k).wait_recv()
            for k in (1, 2, 3):
                w_line(k).wait_send()
            w_core.start()

        @pl.when(r >= 1)
        def _():
            mix_row(r - 1)

        return carry

    loads[5].wait()
    fout_copy.wait_recv()
    lax.fori_loop(0, 5, row_step, 0)

    merged = macc[...].astype(BF)
    mg[0] = merged[0:16]
    mg[1] = merged[16:32]
    gb[z, c] = mg[c]

    def g_copy(k):
        to_z = lax.rem(z + lax.div(k, 2), 8)
        to_c = lax.rem(c + lax.rem(k, 2), 2)
        return remote(
            mg.at[to_c], gb.at[z, c], g_send.at[k], g_recv.at[k], dev(to_z, y, 2 * xh + to_c, core)
        )

    def loop(low, high, action):
        def step(k, carry):
            action(k)
            return carry

        lax.fori_loop(low, high, step, 0)

    loop(1, 16, lambda k: g_copy(k).start())

    prow = iota((256, 256), 0)
    plane_ = iota((256, 256), 1)
    inner = lax.rem(prow, 32)
    column = 24 * lax.div(prow, 32) + inner
    target = jnp.where(plane_ < 128, plane_ + 64, jnp.where(plane_ < 192, plane_ - 128, -1))
    select = ((inner < 24) & (column == target)).astype(F32).astype(BF)
    half = iota((128, 128), 1) < 64

    gain_copy.wait_recv()
    w_core.wait_recv()
    loop(1, 16, lambda k: g_copy(k).wait_recv())
    x0 = gb[:, 0].reshape(128, 512).astype(F32)
    x1 = gb[:, 1].reshape(128, 512).astype(F32)
    square = jnp.sum(x0 * x0, axis=-1, keepdims=True) + jnp.sum(x1 * x1, axis=-1, keepdims=True)
    factor = lax.rsqrt(square * (1.0 / 1024.0) + EPSILON)
    s0 = (x0 * gain_v[0, 0:1, :]).astype(BF)
    s1 = (x1 * gain_v[1, 0:1, :]).astype(BF)
    for g in range(2):
        weights = [
            jnp.concatenate(
                [wb[j % 2, 2 * g + j // 4, 2 * ((j // 2) % 2) + cc] for j in range(8)], axis=0
            )
            for cc in range(2)
        ]
        qkv = (dot_t(s0, weights[0]) + dot_t(s1, weights[1])) * factor
        qkv = dot(qkv.astype(BF), select)
        kv = qkv[:, :128]
        mean = jnp.sum(jnp.where(half, kv * kv, 0.0), axis=-1, keepdims=True) * (1.0 / 64.0)
        kvs[g] = jnp.where(half, kv * (lax.rsqrt(mean + EPSILON) * 0.125), kv).astype(BF)
        query = qkv[:, 128:]
        mean = jnp.sum(query * query, axis=-1, keepdims=True) * (1.0 / 64.0)
        scale = coarse_scales[2 * z + g] * (LOG2E / 8.0)
        qsend[g] = (query * (lax.rsqrt(mean + EPSILON) * scale)).astype(BF)

    def q_copy(k):
        to_xh = lax.rem(xh + lax.div(k, 2), 2)
        to_c = lax.rem(c + lax.rem(k, 2), 2)
        return remote(
            qsend.at[to_c],
            qb.at[xh, c],
            q_send.at[k],
            q_recv.at[k],
            dev(z, y, 2 * to_xh + to_c, core),
        )

    def kv_copy(k):
        to_y = lax.rem(y + lax.div(k, 2), 4)
        to_c = lax.rem(c + lax.rem(k, 2), 2)
        return remote(
            kvs.at[to_c],
            kvb.at[core, y, c],
            kv_send.at[k],
            kv_recv.at[k],
            dev(z, to_y, 2 * xh + to_c, core),
        )

    def forward(k):
        from_y = lax.rem(y + 4 - k, 4)
        return remote(
            kvb.at[core, from_y], kvb.at[core, from_y], fw_send.at[k], fw_recv.at[k], sibling
        )

    loop(1, 4, lambda k: q_copy(k).start())
    loop(1, 8, lambda k: kv_copy(k).start())
    kvb[core, y, c] = kvs[c]
    qb[xh, c] = qsend[c]
    num[...] = jnp.zeros_like(num)
    den[...] = jnp.zeros_like(den)
    loop(1, 4, lambda k: q_copy(k).wait_recv())

    def attend(which, from_y):
        block = kvb[which, from_y].reshape(256, 128)
        weight = jnp.exp2(dot_t(qb[...].reshape(512, 128), block))
        den[...] += weight[:, :128] + weight[:, 128:]
        num[...] += dot(weight.astype(BF), block)

    def direct(k):
        @pl.when(k > 0)
        def _():
            kv_copy(2 * k).wait_recv()

        kv_copy(2 * k + 1).wait_recv()
        forward(k).start()
        attend(core, lax.rem(y + 4 - k, 4))

    def forwarded(k):
        forward(k).wait_recv()
        attend(1 - core, lax.rem(y + 4 - k, 4))

    loop(0, 4, direct)
    loop(0, 4, forwarded)

    half2 = iota((512, 128), 1) < 64
    result = jnp.where(half2, jnp.sum(den[...], axis=-1, keepdims=True), num[...]).astype(BF)
    for hi in range(2):
        for cc in range(2):
            for zz in range(8):
                start = ((hi * 2 + cc) * 8 + zz) * 16
                ob[hi, zz, 16 * cc : 16 * cc + 16] = result[start : start + 16]

    owner_c = lax.div(z, 4)

    def r_copy(k):
        to_z = lax.rem(z + lax.div(k, 2), 8)
        to_xh = lax.rem(xh + lax.rem(k, 2), 2)
        slot = 2 * lax.rem(z, 4) + c
        return remote(
            ob.at[to_xh, to_z],
            rb.at[slot, xh],
            r_send.at[k],
            r_recv.at[2 * slot + xh],
            dev(to_z, y, 2 * to_xh + owner_c, core),
        )

    mine = owner_c == c

    @pl.when(jnp.logical_not(mine))
    def _():
        r_copy(0).start()

    loop(1, 16, lambda k: r_copy(k).start())

    @pl.when(mine)
    def _():
        rb[2 * lax.rem(z, 4) + c, xh] = ob[xh, z]

    own_slot = jnp.where(mine, 2 * (2 * lax.rem(z, 4) + c) + xh, -1)

    def r_wait(s):
        @pl.when(s != own_slot)
        def _():
            remote(
                ob.at[0, 0],
                rb.at[lax.div(s, 2), lax.rem(s, 2)],
                r_send.at[0],
                r_recv.at[s],
                partner,
            ).wait_recv()

    loop(0, 16, r_wait)
    half3 = iota((32, 128), 1) < 64
    for p in range(4):
        even = rb[2 * p, 0].astype(F32) + rb[2 * p, 1].astype(F32)
        odd = rb[2 * p + 1, 0].astype(F32) + rb[2 * p + 1, 1].astype(F32)
        upper = jnp.where(half3, pltpu.roll(even, 64, 1), odd)
        lower = jnp.where(half3, even, pltpu.roll(odd, 64, 1))
        cv_v[:, 128 * p : 128 * p + 128] = (upper / lower).astype(BF)
    cv_copy = pltpu.make_async_copy(cv_v, coarse_out.at[0], load_sem.at[0])
    cv_copy.start()

    for copy in slow_copies + fast_copies + [fout_copy, gain_copy, w_core]:
        copy.wait_send()
    for k in (1, 2, 3):
        w_plane(k).wait_send()

    def finish_row(r):
        att_copy(r).wait_send()
        fine_copy(r).wait()

    loop(0, 4, finish_row)
    loop(1, 16, lambda k: g_copy(k).wait_send())
    loop(1, 4, lambda k: q_copy(k).wait_send())
    loop(1, 8, lambda k: kv_copy(k).wait_send())
    loop(0, 4, lambda k: forward(k).wait_send())

    @pl.when(jnp.logical_not(mine))
    def _():
        r_copy(0).wait_send()

    loop(1, 16, lambda k: r_copy(k).wait_send())
    cv_copy.wait()


def shards(
    image,
    timestep,
    class_label,
    class_table,
    fine_modulation,
    coarse_modulation,
    fine_project,
    fine_output,
    fine_scales,
    merge_weight,
    coarse_project,
    coarse_scales,
):
    smem = pl.BlockSpec(memory_space=pltpu.SMEM)
    hbm = pl.BlockSpec(memory_space=pl.ANY)
    vmem = pltpu.VMEM
    dma = pltpu.SemaphoreType.DMA
    return pl.pallas_call(
        kernel,
        out_shape=(
            jax.ShapeDtypeStruct((4, 128, 256), BF),
            jax.ShapeDtypeStruct((1, 32, 512), BF),
        ),
        in_specs=[smem] * 4 + [hbm] * 8,
        out_specs=(hbm, hbm),
        scratch_shapes=[
            vmem((10, 128, 512), BF),
            vmem((1000, 256), BF),
            vmem((256, 512), BF),
            vmem((256, 512), BF),
            vmem((512, 768), BF),
            vmem((512, 768), BF),
            vmem((2, 256, 512), BF),
            vmem((4, 2048, 512), BF),
            vmem((512, 24), BF),
            vmem((4, 512, 256), BF),
            vmem((10, 128, 256), BF),
            vmem((10, 128, 256), BF),
            vmem((4, 128, 256), BF),
            vmem((4, 128, 256), BF),
            vmem((4, 128, 256), BF),
            vmem((32, 512), F32),
            vmem((2, 16, 512), BF),
            vmem((8, 2, 16, 512), BF),
            vmem((2, 8, 512), F32),
            vmem((2, 4, 4, 32, 512), BF),
            vmem((2, 128, 128), BF),
            vmem((2, 128, 128), BF),
            vmem((2, 4, 2, 128, 128), BF),
            vmem((2, 2, 128, 128), BF),
            vmem((512, 128), F32),
            vmem((512, 128), F32),
            vmem((2, 8, 32, 128), BF),
            vmem((8, 2, 32, 128), BF),
            vmem((32, 512), BF),
            dma((10,)),
            dma((4,)),
            dma((6,)),
            dma((6,)),
            dma((2,)),
            dma((2,)),
            dma((4,)),
            dma((4,)),
            dma((4,)),
            dma((7,)),
            dma((7,)),
            dma((16,)),
            dma((16,)),
            dma((8,)),
            dma((8,)),
            dma((4,)),
            dma((4,)),
            dma((4,)),
            dma((4,)),
            dma((16,)),
            dma((16,)),
        ],
        compiler_params=pltpu.CompilerParams(
            collective_id=0, has_side_effects=True, vmem_limit_bytes=48 * 1024 * 1024
        ),
    )(
        timestep,
        class_label,
        fine_scales,
        coarse_scales,
        image,
        class_table,
        fine_modulation,
        coarse_modulation,
        fine_project,
        fine_output,
        merge_weight.reshape(4, 2048, 512),
        coarse_project,
    )


def solution(mesh):
    in_specs = (
        P("band", None, None),
        P(),
        P(),
        P(),
        P(),
        P(None, "col"),
        P(None, "col"),
        P("col", None),
        P(),
        P(None, "col"),
        P("col", "band"),
        P(),
    )
    out_specs = (P("band", None, "col"), P("band", None, "col"))
    return jax.shard_map(shards, mesh=mesh, in_specs=in_specs, out_specs=out_specs, check_vma=False)
```

```python
import math

import jax
import jax.numpy as jnp
from jax import lax
from jax.experimental import pallas as pl
from jax.experimental.pallas import tpu as pltpu
from jax.sharding import PartitionSpec as P

EPSILON = 1e-06
LOG2E = math.log2(math.e)
BF = jnp.bfloat16
F32 = jnp.float32
MESH = pl.DeviceIdType.MESH
BANDS = 128


def dot(a, b):
    return jnp.dot(a, b, preferred_element_type=F32)


def dot_t(a, b):
    return lax.dot_general(a, b, (((1,), (1,)), ((), ())), preferred_element_type=F32)


def iota(shape, dim):
    return lax.broadcasted_iota(jnp.int32, shape, dim)


def kernel(
    timestep_h,
    label_h,
    fine_scales_h,
    coarse_scales_h,
    image,
    class_table,
    fine_modulation,
    coarse_modulation,
    fine_project,
    fine_output,
    merge_weight,
    coarse_project,
    fine_out,
    coarse_out,
    xb,
    table_v,
    fmod_v,
    cmod_v,
    fproj_v,
    wperm,
    fout_v,
    merge_v,
    cproj_v,
    qs,
    kb,
    vb,
    att_own,
    att_got,
    fine_v,
    mg,
    gb,
    gain_v,
    wst,
    wb,
    kvs,
    qsend,
    kvb,
    qb,
    num,
    den,
    ob,
    rb,
    cv_v,
    timestep,
    label,
    fine_scales,
    coarse_scales,
    entered,
    load_sem,
    merge_sem,
    halo_send,
    halo_recv,
    pair_send,
    pair_recv,
    att_send,
    att_recv,
    fine_sem,
    w_send,
    w_recv,
    g_send,
    g_recv,
    kv_send,
    kv_recv,
    q_send,
    q_recv,
    fw_send,
    fw_recv,
    r_send,
    r_recv,
):
    band = lax.axis_index("band")
    c = lax.axis_index("col")
    core = lax.rem(band, 2)
    xh = lax.rem(lax.div(band, 2), 2)
    y = lax.rem(lax.div(band, 4), 4)
    z = lax.div(band, 16)
    x = 2 * xh + c

    def dev(zz, yy, xx, kk):
        return (((zz * 4 + yy) * 2 + lax.div(xx, 2)) * 2 + kk, lax.rem(xx, 2))

    sibling = dev(z, y, x, 1 - core)
    partner = (band, 1 - c)
    slow = (lax.rem(band + BANDS - 1 + 2 * core, BANDS), 1 - c)

    def row_of(u):
        return u + (1 - core) * (3 - 2 * u)

    def load(src, dst, k):
        return pltpu.make_async_copy(src, dst, load_sem.at[k])

    loads = [
        load(fine_modulation, fmod_v, 4),
        load(class_table, table_v, 5),
        load(fine_project, fproj_v, 6),
        load(coarse_modulation, cmod_v, 7),
        load(coarse_project, cproj_v, 8),
        load(fine_output, fout_v.at[c], 9),
    ]
    scalars = [
        load(timestep_h, timestep, 10),
        load(label_h, label, 11),
        load(fine_scales_h, fine_scales, 12),
        load(coarse_scales_h, coarse_scales, 13),
    ]
    for copy in scalars:
        copy.start()
    rows = [load(image.at[row_of(u)], xb.at[3 + u], u) for u in range(4)]
    merges = [
        pltpu.make_async_copy(merge_weight.at[row_of(u)], merge_v.at[u], merge_sem.at[u])
        for u in range(4)
    ]
    for copy in loads[:3]:
        copy.start()
    for copy in rows:
        copy.start()
    for copy in loads[3:]:
        copy.start()

    barrier = pltpu.get_barrier_semaphore()

    def signal(device):
        pl.semaphore_signal(barrier, inc=1, device_id=device, device_id_type=MESH)

    def near(dz, dy, dx):
        return dev(lax.rem(z + 8 + dz, 8), lax.rem(y + 4 + dy, 4), lax.rem(x + 4 + dx, 4), core)

    nearest = [near(*d) for d in ((0, 0, 1), (0, 0, -1), (0, 1, 0), (0, -1, 0), (1, 0, 0), (-1, 0, 0))]
    for device in [slow, sibling] + nearest:
        signal(device)

    move_z = lax.rem(2 * z + lax.div(y, 2), 8)
    move_y = 2 * lax.div(z, 4) + lax.rem(y, 2)
    moves = (move_z != z) | (move_y != y)
    mover = dev(move_z, move_y, x, core)

    pl.semaphore_wait(barrier, 8)

    def vouch(step, devices):
        for device in devices:
            pl.semaphore_signal(
                entered.at[step], inc=1, device_id=device, device_id_type=MESH
            )

    pending = []

    def loop(low, high, action):
        def step(k, carry):
            action(k)
            return carry

        lax.fori_loop(low, high, step, 0)

    def remote(src, dst, send, recv, device):
        return pltpu.make_async_remote_copy(
            src_ref=src,
            dst_ref=dst,
            send_sem=send,
            recv_sem=recv,
            device_id=device,
            device_id_type=MESH,
        )

    slow_copies = [
        remote(
            image.at[row_of(3 - j)], xb.at[7 + j], halo_send.at[j], halo_recv.at[j], slow
        )
        for j in range(3)
    ]
    fast_copies = [
        remote(
            image.at[row_of(j)], xb.at[2 - j], halo_send.at[3 + j], halo_recv.at[3 + j], sibling
        )
        for j in range(3)
    ]
    for copy in slow_copies + fast_copies:
        copy.start()
    pending.extend(copy.wait_send for copy in slow_copies + fast_copies)
    fout_copy = remote(
        fine_output.at[core], fout_v.at[c, core], pair_send.at[0], pair_recv.at[0], partner
    )
    fout_pass = remote(
        fout_v.at[1 - c, core],
        fout_v.at[1 - c, core],
        pair_send.at[2],
        pair_recv.at[2],
        sibling,
    )
    fout_copy.start()
    pending.append(fout_copy.wait_send)
    vouch(0, nearest)
    for copy in merges:
        copy.start()

    loads[4].wait()
    wst[...] = jnp.concatenate(
        [cproj_v[...].astype(F32), jnp.zeros((8, 512), F32)], axis=0
    ).astype(BF)
    w_move = remote(wst, wb.at[core, move_y, x], w_send.at[7], w_recv.at[7], mover)

    @pl.when(jnp.logical_not(moves))
    def _():
        wb[core, y, x] = wst[...]

    def w_move_done():
        @pl.when(moves)
        def _():
            w_move.wait_send()

    pending.append(w_move_done)

    def w_line(k):
        return remote(
            wb.at[core, y, x],
            wb.at[core, y, x],
            w_send.at[k],
            w_recv.at[k],
            dev(z, y, lax.rem(x + k, 4), core),
        )

    def w_plane(k):
        return remote(
            wb.at[core, y],
            wb.at[core, y],
            w_send.at[3 + k],
            w_recv.at[3 + k],
            dev(z, lax.rem(y + k, 4), x, core),
        )

    w_core = remote(wb.at[core], wb.at[core], w_send.at[0], w_recv.at[0], sibling)
    for copy in scalars:
        copy.wait()
    lane = iota((8, 256), 1)
    freq = jnp.exp((-math.log(10000.0) / 128.0) * lax.rem(lane, 128).astype(F32))
    angle = timestep[0].astype(F32) * freq
    time = jnp.where(lane < 128, jnp.cos(angle), jnp.sin(angle))
    one_hot = (iota((8, 1000), 1) == label[0]).astype(F32).astype(BF)
    loads[1].wait()
    condition = dot(one_hot, table_v[...]) + time
    c_hi = condition.astype(BF)
    rest = condition - c_hi.astype(F32)
    c_mid = rest.astype(BF)
    c_lo = (rest - c_mid.astype(F32)).astype(BF)

    def gain_of(weights):
        return 1.0 + (dot(c_hi, weights) + (dot(c_mid, weights) + dot(c_lo, weights)))

    loads[0].wait()
    fine_gain = gain_of(fmod_v[...])[0:1, :]
    loads[3].wait()
    gain_v[c] = gain_of(cmod_v[...])
    gain_copy = remote(gain_v.at[c], gain_v.at[c], pair_send.at[1], pair_recv.at[1], partner)
    gain_copy.start()
    pending.append(gain_copy.wait_send)

    pl.semaphore_wait(entered.at[0], 6)
    vouch(1, [near(2, 0, 0), near(-2, 0, 0), near(0, 2, 0)])

    loads[2].wait()
    fp = fproj_v[...]
    for part in range(3):
        for h in range(4):
            wperm[:, 256 * part + 64 * h : 256 * part + 64 * h + 64] = fp[
                :, 192 * h + 64 * part : 192 * h + 64 * part + 64
            ]
    ones_block = (lax.div(iota((256, 256), 0), 64) == lax.div(iota((256, 256), 1), 64)).astype(
        F32
    ).astype(BF)
    lane_head = lax.div(iota((1, 256), 1), 64)
    q_scale = jnp.zeros((1, 256), F32)
    for h in range(4):
        q_scale = jnp.where(lane_head == h, fine_scales[4 * c + h] * (LOG2E / 8.0), q_scale)

    def unit_factor(u):
        sq = u * u
        hi = sq.astype(BF)
        lo = (sq - hi.astype(F32)).astype(BF)
        return lax.rsqrt((dot(hi, ones_block) + dot(lo, ones_block)) * (1.0 / 64.0) + EPSILON)

    def normed_of(pixels):
        wide = pixels.astype(F32)
        mean = jnp.mean(wide * wide, axis=-1, keepdims=True)
        return (wide * lax.rsqrt(mean + EPSILON) * fine_gain).astype(BF)

    def keys_values(normed):
        kv = dot(normed, wperm[:, 256:768]).astype(BF)
        key = kv[:, :256].astype(F32)
        return (key * unit_factor(key) * 0.125).astype(BF), kv[:, 256:]

    for copy in rows:
        copy.wait()
    normed = normed_of(xb[3:7].reshape(512, 512))
    key, value = keys_values(normed)
    kb[3:7] = key.reshape(4, 128, 256)
    vb[3:7] = value.reshape(4, 128, 256)
    query = dot(normed, wperm[:, 0:256]).astype(BF).astype(F32)
    query = query * unit_factor(query) * q_scale
    for h in range(4):
        masked = jnp.where(lane_head == h, query, 0.0).astype(BF).reshape(4, 4, 32, 256)
        qs[:, :, 32 * h : 32 * h + 32, :] = masked
    pl.semaphore_wait(entered.at[1], 3)
    vouch(2, [near(0, 0, 1), near(0, 0, -1), near(0, 0, 2), near(0, 2, 0)])
    for copy in fast_copies:
        copy.wait_recv()
    key, value = keys_values(normed_of(xb[0:3].reshape(384, 512)))
    kb[0:3] = key.reshape(3, 128, 256)
    vb[0:3] = value.reshape(3, 128, 256)

    first = (0, 16, 48, 64)
    column_gap = iota((32, 448), 0) - lax.rem(iota((32, 448), 1), 64)
    far = []
    for b in range(4):
        gap = column_gap + (32 * b - first[b])
        far.append(jnp.where((gap <= 3) & (gap >= -3), 0.0, -1e30))
    key_row = lax.div(iota((1, 448), 1), 64) - 3
    perm = (iota((128, 128), 1) == 4 * lax.rem(iota((128, 128), 0), 32) + lax.div(iota((128, 128), 0), 32)).astype(F32).astype(BF)

    def att_copy(r):
        return remote(att_own.at[r], att_got.at[r], att_send.at[r], att_recv.at[r], partner)

    def fine_copy(r):
        return pltpu.make_async_copy(fine_v.at[r], fine_out.at[row_of(r)], fine_sem.at[r])

    def attend_row(r):
        slot = key_row + r
        row = 4 * band + slot + (1 - core) * (3 - 2 * slot)
        outside = jnp.where((row < 0) | (row >= 4 * BANDS), -1e30, 0.0)
        for b in range(4):
            keys = kb[pl.ds(r, 7), first[b] : first[b] + 64].reshape(448, 256)
            values = vb[pl.ds(r, 7), first[b] : first[b] + 64].reshape(448, 256)
            logits = dot_t(qs[r, b], keys).reshape(4, 32, 448) + (far[b] + outside)[None]
            weight = jnp.exp2(logits)
            total = jnp.sum(weight, axis=-1, keepdims=True)
            out = dot(weight.astype(BF).reshape(128, 448), values).reshape(4, 32, 256)
            out = out * (1.0 / total)
            mixed = jnp.zeros((32, 256), F32)
            for h in range(4):
                mixed = jnp.where(lane_head == h, out[h], mixed)
            att_own[r, 32 * b : 32 * b + 32] = mixed.astype(BF)
        att_copy(r).start()

    def mix_row(r):
        full = xb[3 + r].astype(F32) + dot(att_own[r], fout_v[c].reshape(256, 512))
        full = full + dot(att_got[r], fout_v[1 - c].reshape(256, 512))
        fine_v[r] = jnp.where(c == 0, full[:, :256], full[:, 256:]).astype(BF)
        patches = dot(perm, full.astype(BF)).astype(BF)
        part = jnp.zeros((32, 512), F32)
        for p in range(4):
            part = part + dot(patches[32 * p : 32 * p + 32], merge_v[r, 512 * p : 512 * p + 512, :])
        return part

    def new_row(r):
        slow_copies[r - 1].wait_recv()
        key, value = keys_values(normed_of(xb[6 + r]))
        kb[6 + r] = key
        vb[6 + r] = value

    attend_row(0)
    pl.semaphore_wait(entered.at[2], 4)

    @pl.when(moves)
    def _():
        w_move.start()

    loads[5].wait()
    fout_copy.wait_recv()
    fout_pass.start()
    pending.append(fout_pass.wait_send)
    new_row(1)
    attend_row(1)

    @pl.when(moves)
    def _():
        w_move.wait_recv()

    for k in (2, 1, 3):
        w_line(k).start()
    new_row(2)
    attend_row(2)
    for k in (1, 2, 3):
        w_line(k).wait_recv()
    for k in (2, 1, 3):
        w_plane(k).start()
    new_row(3)
    attend_row(3)
    fout_pass.wait_recv()
    for copy in merges:
        copy.wait()
    for r in range(3):
        att_copy(r).wait_recv()
    merged = mix_row(0) + mix_row(1) + mix_row(2)
    att_copy(3).wait_recv()
    merged = (merged + mix_row(3)).astype(BF)
    pending.extend(w_plane(k).wait_send for k in (1, 2, 3))

    def finish_row(r):
        att_copy(r).wait_send()
        fine_copy(r).wait()

    pending.append(lambda: loop(0, 4, finish_row))

    mg[0] = merged[0:16]
    mg[1] = merged[16:32]
    gb[z, c] = mg[c]

    def g_copy(k):
        to_z = lax.rem(z + lax.div(k, 2), 8)
        to_c = lax.rem(c + lax.rem(k, 2), 2)
        return remote(
            mg.at[to_c], gb.at[z, c], g_send.at[k], g_recv.at[k], dev(to_z, y, 2 * xh + to_c, core)
        )

    loop(1, 16, lambda k: g_copy(k).start())
    for k in (1, 2, 3):
        w_plane(k).wait_recv()
    for k in (1, 2, 3):
        w_line(k).wait_send()
    w_core.start()
    pending.append(w_core.wait_send)
    pending.append(lambda: loop(1, 16, lambda k: g_copy(k).wait_send()))
    for r in range(4):
        fine_copy(r).start()

    prow = iota((256, 256), 0)
    plane_ = iota((256, 256), 1)
    inner = lax.rem(prow, 32)
    column = 24 * lax.div(prow, 32) + inner
    target = jnp.where(plane_ < 128, plane_ + 64, jnp.where(plane_ < 192, plane_ - 128, -1))
    select = ((inner < 24) & (column == target)).astype(F32).astype(BF)
    half = iota((128, 128), 1) < 64

    gain_copy.wait_recv()
    w_core.wait_recv()
    loop(1, 16, lambda k: g_copy(k).wait_recv())
    x0 = gb[:, 0].reshape(128, 512).astype(F32)
    x1 = gb[:, 1].reshape(128, 512).astype(F32)
    square = jnp.sum(x0 * x0, axis=-1, keepdims=True) + jnp.sum(x1 * x1, axis=-1, keepdims=True)
    factor = lax.rsqrt(square * (1.0 / 1024.0) + EPSILON)
    s0 = (x0 * gain_v[0, 0:1, :]).astype(BF)
    s1 = (x1 * gain_v[1, 0:1, :]).astype(BF)
    for g in range(2):
        weights = [
            jnp.concatenate(
                [wb[j % 2, 2 * g + j // 4, 2 * ((j // 2) % 2) + cc] for j in range(8)], axis=0
            )
            for cc in range(2)
        ]
        qkv = (dot_t(s0, weights[0]) + dot_t(s1, weights[1])) * factor
        qkv = dot(qkv.astype(BF), select)
        kv = qkv[:, :128]
        mean = jnp.sum(jnp.where(half, kv * kv, 0.0), axis=-1, keepdims=True) * (1.0 / 64.0)
        kvs[g] = jnp.where(half, kv * (lax.rsqrt(mean + EPSILON) * 0.125), kv).astype(BF)
        query = qkv[:, 128:]
        mean = jnp.sum(query * query, axis=-1, keepdims=True) * (1.0 / 64.0)
        scale = coarse_scales[z + 8 * g] * (LOG2E / 8.0)
        qsend[g] = (query * (lax.rsqrt(mean + EPSILON) * scale)).astype(BF)

    def q_copy(k):
        to_xh = lax.rem(xh + lax.div(k, 2), 2)
        to_c = lax.rem(c + lax.rem(k, 2), 2)
        return remote(
            qsend.at[to_c],
            qb.at[xh, c],
            q_send.at[k],
            q_recv.at[k],
            dev(z, y, 2 * to_xh + to_c, core),
        )

    def kv_copy(k):
        to_y = lax.rem(y + lax.div(k, 2), 4)
        to_c = lax.rem(c + lax.rem(k, 2), 2)
        return remote(
            kvs.at[to_c],
            kvb.at[core, y, c],
            kv_send.at[k],
            kv_recv.at[k],
            dev(z, to_y, 2 * xh + to_c, core),
        )

    def forward(k):
        from_y = lax.rem(y + 4 - k, 4)
        return remote(
            kvb.at[core, from_y], kvb.at[core, from_y], fw_send.at[k], fw_recv.at[k], sibling
        )

    for k in (4, 5, 2, 3, 6, 7, 1):
        kv_copy(k).start()
    loop(1, 4, lambda k: q_copy(k).start())
    pending.append(lambda: loop(1, 4, lambda k: q_copy(k).wait_send()))
    pending.append(lambda: loop(1, 8, lambda k: kv_copy(k).wait_send()))
    kvb[core, y, c] = kvs[c]
    qb[xh, c] = qsend[c]
    num[...] = jnp.zeros_like(num)
    den[...] = jnp.zeros_like(den)
    loop(1, 4, lambda k: q_copy(k).wait_recv())

    def attend(which, from_y):
        block = kvb[which, from_y].reshape(256, 128)
        weight = jnp.exp2(dot_t(qb[...].reshape(512, 128), block))
        den[...] += weight[:, :128] + weight[:, 128:]
        num[...] += dot(weight.astype(BF), block)

    def direct(k):
        @pl.when(k > 0)
        def _():
            kv_copy(2 * k).wait_recv()

        kv_copy(2 * k + 1).wait_recv()
        forward(k).start()
        attend(core, lax.rem(y + 4 - k, 4))

    def forwarded(k):
        forward(k).wait_recv()
        attend(1 - core, lax.rem(y + 4 - k, 4))

    loop(0, 4, direct)
    loop(0, 4, forwarded)
    pending.append(lambda: loop(0, 4, lambda k: forward(k).wait_send()))

    half2 = iota((512, 128), 1) < 64
    result = jnp.where(half2, jnp.sum(den[...], axis=-1, keepdims=True), num[...]).astype(BF)
    for hi in range(2):
        for cc in range(2):
            for zz in range(8):
                start = ((hi * 2 + cc) * 8 + zz) * 16
                ob[hi, zz, 16 * cc : 16 * cc + 16] = result[start : start + 16]

    def r_copy(k):
        to_z = lax.rem(z + lax.div(k, 2), 8)
        to_xh = lax.rem(xh + lax.rem(k, 2), 2)
        return remote(
            ob.at[to_xh, to_z],
            rb.at[z, xh],
            r_send.at[k],
            r_recv.at[k],
            dev(to_z, y, 2 * to_xh + c, core),
        )

    def r_from(k):
        from_z = lax.rem(z + 8 - lax.div(k, 2), 8)
        from_xh = lax.rem(xh + lax.rem(k, 2), 2)
        return remote(
            ob.at[from_xh, from_z],
            rb.at[from_z, from_xh],
            r_send.at[k],
            r_recv.at[k],
            dev(from_z, y, 2 * from_xh + c, core),
        )

    loop(1, 16, lambda k: r_copy(k).start())
    pending.append(lambda: loop(1, 16, lambda k: r_copy(k).wait_send()))
    rb[z, xh] = ob[xh, z]
    loop(1, 16, lambda k: r_from(k).wait_recv())
    half3 = iota((32, 128), 1) < 64
    for p in range(4):
        even = rb[2 * p, 0].astype(F32) + rb[2 * p, 1].astype(F32)
        odd = rb[2 * p + 1, 0].astype(F32) + rb[2 * p + 1, 1].astype(F32)
        upper = jnp.where(half3, pltpu.roll(even, 64, 1), odd)
        lower = jnp.where(half3, even, pltpu.roll(odd, 64, 1))
        cv_v[:, 128 * p : 128 * p + 128] = (upper / lower).astype(BF)
    cv_copy = pltpu.make_async_copy(cv_v, coarse_out.at[0], load_sem.at[0])
    cv_copy.start()

    pending.append(cv_copy.wait)
    for wait in pending:
        wait()


def shards(
    image,
    timestep,
    class_label,
    class_table,
    fine_modulation,
    coarse_modulation,
    fine_project,
    fine_output,
    fine_scales,
    merge_weight,
    coarse_project,
    coarse_scales,
):
    hbm = pl.BlockSpec(memory_space=pl.ANY)
    vmem = pltpu.VMEM
    smem = pltpu.SMEM
    dma = pltpu.SemaphoreType.DMA
    return pl.pallas_call(
        kernel,
        out_shape=(
            jax.ShapeDtypeStruct((4, 128, 256), BF),
            jax.ShapeDtypeStruct((1, 32, 512), BF),
        ),
        in_specs=[hbm] * 12,
        out_specs=(hbm, hbm),
        scratch_shapes=[
            vmem((10, 128, 512), BF),
            vmem((1000, 256), BF),
            vmem((256, 512), BF),
            vmem((256, 512), BF),
            vmem((512, 768), BF),
            vmem((512, 768), BF),
            vmem((2, 2, 128, 512), BF),
            vmem((4, 2048, 512), BF),
            vmem((24, 512), BF),
            vmem((4, 4, 128, 256), BF),
            vmem((10, 128, 256), BF),
            vmem((10, 128, 256), BF),
            vmem((4, 128, 256), BF),
            vmem((4, 128, 256), BF),
            vmem((4, 128, 256), BF),
            vmem((2, 16, 512), BF),
            vmem((8, 2, 16, 512), BF),
            vmem((2, 8, 512), F32),
            vmem((32, 512), BF),
            vmem((2, 4, 4, 32, 512), BF),
            vmem((2, 128, 128), BF),
            vmem((2, 128, 128), BF),
            vmem((2, 4, 2, 128, 128), BF),
            vmem((2, 2, 128, 128), BF),
            vmem((512, 128), F32),
            vmem((512, 128), F32),
            vmem((2, 8, 32, 128), BF),
            vmem((8, 2, 32, 128), BF),
            vmem((32, 512), BF),
            smem((1,), jnp.int32),
            smem((1,), jnp.int32),
            smem((8,), F32),
            smem((16,), F32),
            pltpu.SemaphoreType.REGULAR((3,)),
            dma((14,)),
            dma((4,)),
            dma((6,)),
            dma((6,)),
            dma((3,)),
            dma((3,)),
            dma((4,)),
            dma((4,)),
            dma((4,)),
            dma((8,)),
            dma((8,)),
            dma((16,)),
            dma((16,)),
            dma((8,)),
            dma((8,)),
            dma((4,)),
            dma((4,)),
            dma((4,)),
            dma((4,)),
            dma((16,)),
            dma((16,)),
        ],
        compiler_params=pltpu.CompilerParams(
            collective_id=0, has_side_effects=True, vmem_limit_bytes=62 * 1024 * 1024
        ),
    )(
        timestep,
        class_label,
        fine_scales,
        coarse_scales,
        image,
        class_table,
        fine_modulation,
        coarse_modulation,
        fine_project,
        fine_output.reshape(2, 128, 512),
        merge_weight.reshape(4, 2048, 512),
        coarse_project.T,
    )


def solution(mesh):
    in_specs = (
        P("band", None, None),
        P(),
        P(),
        P(),
        P(),
        P(None, "col"),
        P(None, "col"),
        P("col", None),
        P(),
        P(None, "col"),
        P("col", "band"),
        P(),
    )
    out_specs = (P("band", None, "col"), P("band", None, "col"))
    return jax.shard_map(shards, mesh=mesh, in_specs=in_specs, out_specs=out_specs, check_vma=False)
```

```python
import math

import jax
import jax.numpy as jnp
from jax import lax
from jax.experimental import pallas as pl
from jax.experimental.pallas import tpu as pltpu
from jax.sharding import PartitionSpec as P

EPSILON = 1e-06
LOG2E = math.log2(math.e)
BF = jnp.bfloat16
F32 = jnp.float32
MESH = pl.DeviceIdType.MESH
BANDS = 128


def dot(a, b):
    return jnp.dot(a, b, preferred_element_type=F32)


def dot_t(a, b):
    return lax.dot_general(a, b, (((1,), (1,)), ((), ())), preferred_element_type=F32)


def iota(shape, dim):
    return lax.broadcasted_iota(jnp.int32, shape, dim)


def kernel(
    timestep_h,
    label_h,
    fine_scales_h,
    coarse_scales_h,
    image,
    class_table,
    fine_modulation,
    coarse_modulation,
    fine_project,
    fine_output,
    merge_weight,
    coarse_project,
    fine_out,
    coarse_out,
    xb,
    table_v,
    fmod_v,
    cmod_v,
    fproj_v,
    wperm,
    fout_v,
    merge_v,
    cproj_v,
    qs,
    kb,
    vb,
    att_own,
    att_got,
    mg,
    gb,
    gain_v,
    wb,
    kvs,
    qsend,
    kvb,
    qb,
    num,
    den,
    ob,
    rb,
    timestep,
    label,
    fine_scales,
    coarse_scales,
    entered,
    load_sem,
    merge_sem,
    halo_send,
    halo_recv,
    pair_send,
    pair_recv,
    att_send,
    att_recv,
    fine_sem,
    w_send,
    w_recv,
    g_send,
    g_recv,
    kv_send,
    kv_recv,
    q_send,
    q_recv,
    fw_send,
    fw_recv,
    r_send,
    r_recv,
):
    band = lax.axis_index("band")
    c = lax.axis_index("col")
    core = lax.rem(band, 2)
    xh = lax.rem(lax.div(band, 2), 2)
    y = lax.rem(lax.div(band, 4), 4)
    z = lax.div(band, 16)
    x = 2 * xh + c

    def dev(zz, yy, xx, kk):
        return (((zz * 4 + yy) * 2 + lax.div(xx, 2)) * 2 + kk, lax.rem(xx, 2))

    sibling = dev(z, y, x, 1 - core)
    partner = (band, 1 - c)
    slow = (lax.rem(band + BANDS - 1 + 2 * core, BANDS), 1 - c)

    def row_of(u):
        return u + (1 - core) * (3 - 2 * u)

    def load(src, dst, k):
        return pltpu.make_async_copy(src, dst, load_sem.at[k])

    loads = [
        load(fine_modulation, fmod_v, 4),
        load(class_table, table_v, 5),
        load(fine_project, fproj_v, 6),
        load(coarse_modulation, cmod_v, 7),
        load(coarse_project, cproj_v, 8),
        load(fine_output, fout_v.at[c], 9),
    ]
    scalars = [
        load(timestep_h, timestep, 10),
        load(label_h, label, 11),
        load(fine_scales_h, fine_scales, 12),
        load(coarse_scales_h, coarse_scales, 13),
    ]
    for copy in scalars:
        copy.start()
    rows = [load(image.at[row_of(u)], xb.at[3 + u], u) for u in range(4)]
    merges = [
        pltpu.make_async_copy(merge_weight.at[row_of(u)], merge_v.at[u], merge_sem.at[u])
        for u in range(4)
    ]
    for copy in loads[:3]:
        copy.start()
    for copy in rows:
        copy.start()
    for copy in loads[3:]:
        copy.start()

    barrier = pltpu.get_barrier_semaphore()

    def signal(device):
        pl.semaphore_signal(barrier, inc=1, device_id=device, device_id_type=MESH)

    def near(dz, dy, dx):
        return dev(lax.rem(z + 8 + dz, 8), lax.rem(y + 4 + dy, 4), lax.rem(x + 4 + dx, 4), core)

    nearest = [near(*d) for d in ((0, 0, 1), (0, 0, -1), (0, 1, 0), (0, -1, 0), (1, 0, 0), (-1, 0, 0))]
    for device in [slow, sibling] + nearest:
        signal(device)

    pl.semaphore_wait(barrier, 8)

    def vouch(step, devices):
        for device in devices:
            pl.semaphore_signal(
                entered.at[step], inc=1, device_id=device, device_id_type=MESH
            )

    pending = []

    def loop(low, high, action):
        def step(k, carry):
            action(k)
            return carry

        lax.fori_loop(low, high, step, 0)

    def remote(src, dst, send, recv, device):
        return pltpu.make_async_remote_copy(
            src_ref=src,
            dst_ref=dst,
            send_sem=send,
            recv_sem=recv,
            device_id=device,
            device_id_type=MESH,
        )

    slow_copies = [
        remote(
            image.at[row_of(3 - j)], xb.at[7 + j], halo_send.at[j], halo_recv.at[j], slow
        )
        for j in range(3)
    ]
    fast_copies = [
        remote(
            image.at[row_of(j)], xb.at[2 - j], halo_send.at[3 + j], halo_recv.at[3 + j], sibling
        )
        for j in range(3)
    ]
    for copy in slow_copies + fast_copies:
        copy.start()
    pending.extend(copy.wait_send for copy in slow_copies + fast_copies)
    fout_copy = remote(
        fine_output.at[core], fout_v.at[c, core], pair_send.at[0], pair_recv.at[0], partner
    )
    fout_pass = remote(
        fout_v.at[1 - c, core],
        fout_v.at[1 - c, core],
        pair_send.at[2],
        pair_recv.at[2],
        sibling,
    )
    fout_copy.start()
    pending.append(fout_copy.wait_send)
    vouch(0, nearest)
    for copy in merges:
        copy.start()

    loads[4].wait()
    wb[core, y, x] = jnp.concatenate(
        [cproj_v[...].astype(F32), jnp.zeros((8, 512), F32)], axis=0
    ).astype(BF)

    def w_line(k):
        return remote(
            wb.at[core, y, x],
            wb.at[core, y, x],
            w_send.at[k],
            w_recv.at[k],
            dev(z, y, lax.rem(x + k, 4), core),
        )

    def w_plane(k):
        return remote(
            wb.at[core, y],
            wb.at[core, y],
            w_send.at[3 + k],
            w_recv.at[3 + k],
            dev(z, lax.rem(y + k, 4), x, core),
        )

    w_core = remote(wb.at[core], wb.at[core], w_send.at[0], w_recv.at[0], sibling)
    for copy in scalars:
        copy.wait()
    lane = iota((8, 256), 1)
    freq = jnp.exp((-math.log(10000.0) / 128.0) * lax.rem(lane, 128).astype(F32))
    angle = timestep[0].astype(F32) * freq
    time = jnp.where(lane < 128, jnp.cos(angle), jnp.sin(angle))
    one_hot = (iota((8, 1000), 1) == label[0]).astype(F32).astype(BF)
    loads[1].wait()
    condition = dot(one_hot, table_v[...]) + time
    c_hi = condition.astype(BF)
    rest = condition - c_hi.astype(F32)
    c_mid = rest.astype(BF)
    c_lo = (rest - c_mid.astype(F32)).astype(BF)

    def gain_of(weights):
        return 1.0 + (dot(c_hi, weights) + (dot(c_mid, weights) + dot(c_lo, weights)))

    loads[0].wait()
    fine_gain = gain_of(fmod_v[...])[0:1, :]
    loads[3].wait()
    gain_v[c] = gain_of(cmod_v[...])
    gain_copy = remote(gain_v.at[c], gain_v.at[c], pair_send.at[1], pair_recv.at[1], partner)
    gain_copy.start()
    pending.append(gain_copy.wait_send)

    loads[2].wait()
    fp = fproj_v[...]
    for part in range(3):
        for h in range(4):
            wperm[:, 256 * part + 64 * h : 256 * part + 64 * h + 64] = fp[
                :, 192 * h + 64 * part : 192 * h + 64 * part + 64
            ]
    ones_block = (lax.div(iota((256, 256), 0), 64) == lax.div(iota((256, 256), 1), 64)).astype(
        F32
    ).astype(BF)
    lane_head = lax.div(iota((1, 256), 1), 64)
    q_scale = jnp.zeros((1, 256), F32)
    for h in range(4):
        q_scale = jnp.where(lane_head == h, fine_scales[4 * c + h] * (LOG2E / 8.0), q_scale)

    def unit_factor(u):
        sq = u * u
        hi = sq.astype(BF)
        lo = (sq - hi.astype(F32)).astype(BF)
        return lax.rsqrt((dot(hi, ones_block) + dot(lo, ones_block)) * (1.0 / 64.0) + EPSILON)

    def normed_of(pixels):
        wide = pixels.astype(F32)
        mean = jnp.mean(wide * wide, axis=-1, keepdims=True)
        return (wide * lax.rsqrt(mean + EPSILON) * fine_gain).astype(BF)

    def keys_values(normed):
        kv = dot(normed, wperm[:, 256:768]).astype(BF)
        key = kv[:, :256].astype(F32)
        return (key * unit_factor(key) * 0.125).astype(BF), kv[:, 256:]

    for copy in rows:
        copy.wait()
    normed = normed_of(xb[3:7].reshape(512, 512))
    key, value = keys_values(normed)
    kb[3:7] = key.reshape(4, 128, 256)
    vb[3:7] = value.reshape(4, 128, 256)
    query = dot(normed, wperm[:, 0:256]).astype(BF).astype(F32)
    query = query * unit_factor(query) * q_scale
    for h in range(4):
        masked = jnp.where(lane_head == h, query, 0.0).astype(BF).reshape(4, 4, 32, 256)
        qs[:, :, 32 * h : 32 * h + 32, :] = masked
    for copy in fast_copies:
        copy.wait_recv()
    key, value = keys_values(normed_of(xb[0:3].reshape(384, 512)))
    kb[0:3] = key.reshape(3, 128, 256)
    vb[0:3] = value.reshape(3, 128, 256)

    first = (0, 16, 48, 64)
    column_gap = iota((32, 448), 0) - lax.rem(iota((32, 448), 1), 64)
    far = []
    for b in range(4):
        gap = column_gap + (32 * b - first[b])
        far.append(jnp.where((gap <= 3) & (gap >= -3), 0.0, -1e30))
    key_row = lax.div(iota((1, 448), 1), 64) - 3
    perm = (iota((128, 128), 1) == 4 * lax.rem(iota((128, 128), 0), 32) + lax.div(iota((128, 128), 0), 32)).astype(F32).astype(BF)

    def att_copy(r):
        return remote(att_own.at[r], att_got.at[r], att_send.at[r], att_recv.at[r], partner)

    def attend_row(r):
        slot = key_row + r
        row = 4 * band + slot + (1 - core) * (3 - 2 * slot)
        outside = jnp.where((row < 0) | (row >= 4 * BANDS), -1e30, 0.0)
        for b in range(4):
            keys = kb[pl.ds(r, 7), first[b] : first[b] + 64].reshape(448, 256)
            values = vb[pl.ds(r, 7), first[b] : first[b] + 64].reshape(448, 256)
            logits = dot_t(qs[r, b], keys).reshape(4, 32, 448) + (far[b] + outside)[None]
            weight = jnp.exp2(logits)
            total = jnp.sum(weight, axis=-1, keepdims=True)
            out = dot(weight.astype(BF).reshape(128, 448), values).reshape(4, 32, 256)
            out = out * (1.0 / total)
            mixed = jnp.zeros((32, 256), F32)
            for h in range(4):
                mixed = jnp.where(lane_head == h, out[h], mixed)
            att_own[r, 32 * b : 32 * b + 32] = mixed.astype(BF)
        att_copy(r).start()

    def mix_row(r):
        full = xb[3 + r].astype(F32) + dot(att_own[r], fout_v[c].reshape(256, 512))
        full = full + dot(att_got[r], fout_v[1 - c].reshape(256, 512))
        fine_out[row_of(r)] = jnp.where(c == 0, full[:, :256], full[:, 256:]).astype(BF)
        patches = dot(perm, full.astype(BF)).astype(BF)
        part = jnp.zeros((32, 512), F32)
        for p in range(4):
            part = part + dot(patches[32 * p : 32 * p + 32], merge_v[r, 512 * p : 512 * p + 512, :])
        return part

    def new_row(r):
        slow_copies[r - 1].wait_recv()
        key, value = keys_values(normed_of(xb[6 + r]))
        kb[6 + r] = key
        vb[6 + r] = value

    attend_row(0)
    pl.semaphore_wait(entered.at[0], 6)
    vouch(1, [near(2, 0, 0), near(-2, 0, 0), near(0, 2, 0)])
    loads[5].wait()
    fout_copy.wait_recv()
    fout_pass.start()
    pending.append(fout_pass.wait_send)
    new_row(1)
    attend_row(1)
    pl.semaphore_wait(entered.at[1], 3)
    vouch(2, [near(0, 0, 1), near(0, 0, -1), near(0, 0, 2)])
    for k in (2, 1, 3):
        w_line(k).start()
    new_row(2)
    attend_row(2)
    new_row(3)
    attend_row(3)
    for k in (1, 2, 3):
        w_line(k).wait_recv()
    for k in (2, 1, 3):
        w_plane(k).start()
    fout_pass.wait_recv()
    for copy in merges:
        copy.wait()
    for r in range(3):
        att_copy(r).wait_recv()
    merged = mix_row(0) + mix_row(1) + mix_row(2)
    att_copy(3).wait_recv()
    merged = (merged + mix_row(3)).astype(BF)
    pl.semaphore_wait(entered.at[2], 3)
    pending.extend(w_plane(k).wait_send for k in (1, 2, 3))

    def finish_row(r):
        att_copy(r).wait_send()

    pending.append(lambda: loop(0, 4, finish_row))

    mg[0] = merged[0:16]
    mg[1] = merged[16:32]
    gb[z, c] = mg[c]

    def g_copy(k):
        to_z = lax.rem(z + lax.div(k, 2), 8)
        to_c = lax.rem(c + lax.rem(k, 2), 2)
        return remote(
            mg.at[to_c], gb.at[z, c], g_send.at[k], g_recv.at[k], dev(to_z, y, 2 * xh + to_c, core)
        )

    loop(1, 16, lambda k: g_copy(k).start())
    for k in (1, 2, 3):
        w_plane(k).wait_recv()
    for k in (1, 2, 3):
        w_line(k).wait_send()
    w_core.start()
    pending.append(w_core.wait_send)
    pending.append(lambda: loop(1, 16, lambda k: g_copy(k).wait_send()))

    prow = iota((256, 256), 0)
    plane_ = iota((256, 256), 1)
    inner = lax.rem(prow, 32)
    column = 24 * lax.div(prow, 32) + inner
    target = jnp.where(plane_ < 128, plane_ + 64, jnp.where(plane_ < 192, plane_ - 128, -1))
    select = ((inner < 24) & (column == target)).astype(F32).astype(BF)
    half = iota((128, 128), 1) < 64

    gain_copy.wait_recv()
    w_core.wait_recv()
    loop(1, 16, lambda k: g_copy(k).wait_recv())
    x0 = gb[:, 0].reshape(128, 512).astype(F32)
    x1 = gb[:, 1].reshape(128, 512).astype(F32)
    square = jnp.sum(x0 * x0, axis=-1, keepdims=True) + jnp.sum(x1 * x1, axis=-1, keepdims=True)
    factor = lax.rsqrt(square * (1.0 / 1024.0) + EPSILON)
    s0 = (x0 * gain_v[0, 0:1, :]).astype(BF)
    s1 = (x1 * gain_v[1, 0:1, :]).astype(BF)
    for g in range(2):
        weights = [
            jnp.concatenate(
                [wb[j % 2, 2 * g + j // 4, 2 * ((j // 2) % 2) + cc] for j in range(8)], axis=0
            )
            for cc in range(2)
        ]
        qkv = (dot_t(s0, weights[0]) + dot_t(s1, weights[1])) * factor
        qkv = dot(qkv.astype(BF), select)
        kv = qkv[:, :128]
        mean = jnp.sum(jnp.where(half, kv * kv, 0.0), axis=-1, keepdims=True) * (1.0 / 64.0)
        kvs[g] = jnp.where(half, kv * (lax.rsqrt(mean + EPSILON) * 0.125), kv).astype(BF)
        query = qkv[:, 128:]
        mean = jnp.sum(query * query, axis=-1, keepdims=True) * (1.0 / 64.0)
        scale = coarse_scales[2 * z + g] * (LOG2E / 8.0)
        qsend[g] = (query * (lax.rsqrt(mean + EPSILON) * scale)).astype(BF)

    def q_copy(k):
        to_xh = lax.rem(xh + lax.div(k, 2), 2)
        to_c = lax.rem(c + lax.rem(k, 2), 2)
        return remote(
            qsend.at[to_c],
            qb.at[xh, c],
            q_send.at[k],
            q_recv.at[k],
            dev(z, y, 2 * to_xh + to_c, core),
        )

    def kv_copy(k):
        to_y = lax.rem(y + lax.div(k, 2), 4)
        to_c = lax.rem(c + lax.rem(k, 2), 2)
        return remote(
            kvs.at[to_c],
            kvb.at[core, y, c],
            kv_send.at[k],
            kv_recv.at[k],
            dev(z, to_y, 2 * xh + to_c, core),
        )

    def forward(k):
        from_y = lax.rem(y + 4 - k, 4)
        return remote(
            kvb.at[core, from_y], kvb.at[core, from_y], fw_send.at[k], fw_recv.at[k], sibling
        )

    for k in (4, 5, 2, 3, 6, 7, 1):
        kv_copy(k).start()
    loop(1, 4, lambda k: q_copy(k).start())
    pending.append(lambda: loop(1, 4, lambda k: q_copy(k).wait_send()))
    pending.append(lambda: loop(1, 8, lambda k: kv_copy(k).wait_send()))
    kvb[core, y, c] = kvs[c]
    qb[xh, c] = qsend[c]
    num[...] = jnp.zeros_like(num)
    den[...] = jnp.zeros_like(den)
    loop(1, 4, lambda k: q_copy(k).wait_recv())

    def attend(which, from_y):
        block = kvb[which, from_y].reshape(256, 128)
        weight = jnp.exp2(dot_t(qb[...].reshape(512, 128), block))
        den[...] += weight[:, :128] + weight[:, 128:]
        num[...] += dot(weight.astype(BF), block)

    def direct(k):
        @pl.when(k > 0)
        def _():
            kv_copy(2 * k).wait_recv()

        kv_copy(2 * k + 1).wait_recv()
        forward(k).start()
        attend(core, lax.rem(y + 4 - k, 4))

    def forwarded(k):
        forward(k).wait_recv()
        attend(1 - core, lax.rem(y + 4 - k, 4))

    loop(0, 4, direct)
    loop(0, 4, forwarded)
    pending.append(lambda: loop(0, 4, lambda k: forward(k).wait_send()))

    half2 = iota((512, 128), 1) < 64
    result = jnp.where(half2, jnp.sum(den[...], axis=-1, keepdims=True), num[...]).astype(BF)
    for hi in range(2):
        for cc in range(2):
            for zz in range(8):
                start = ((hi * 2 + cc) * 8 + zz) * 16
                ob[hi, zz, 16 * cc : 16 * cc + 16] = result[start : start + 16]

    owner_c = lax.div(z, 4)

    def r_copy(k):
        to_z = lax.rem(z + lax.div(k, 2), 8)
        to_xh = lax.rem(xh + lax.rem(k, 2), 2)
        slot = 2 * lax.rem(z, 4) + c
        return remote(
            ob.at[to_xh, to_z],
            rb.at[slot, xh],
            r_send.at[k],
            r_recv.at[2 * slot + xh],
            dev(to_z, y, 2 * to_xh + owner_c, core),
        )

    mine = owner_c == c

    @pl.when(jnp.logical_not(mine))
    def _():
        r_copy(0).start()

    for k in (8, 9, 7, 11, 6, 10, 5, 13, 4, 12, 3, 15, 2, 14, 1):
        r_copy(k).start()

    @pl.when(mine)
    def _():
        rb[2 * lax.rem(z, 4) + c, xh] = ob[xh, z]

    own_slot = jnp.where(mine, 2 * (2 * lax.rem(z, 4) + c) + xh, -1)

    def r_wait(s):
        @pl.when(s != own_slot)
        def _():
            remote(
                ob.at[0, 0],
                rb.at[lax.div(s, 2), lax.rem(s, 2)],
                r_send.at[0],
                r_recv.at[s],
                partner,
            ).wait_recv()

    loop(0, 16, r_wait)

    def finish_returns():
        @pl.when(jnp.logical_not(mine))
        def _():
            r_copy(0).wait_send()

        loop(1, 16, lambda k: r_copy(k).wait_send())

    pending.append(finish_returns)
    half3 = iota((32, 128), 1) < 64
    for p in range(4):
        even = rb[2 * p, 0].astype(F32) + rb[2 * p, 1].astype(F32)
        odd = rb[2 * p + 1, 0].astype(F32) + rb[2 * p + 1, 1].astype(F32)
        upper = jnp.where(half3, pltpu.roll(even, 64, 1), odd)
        lower = jnp.where(half3, even, pltpu.roll(odd, 64, 1))
        coarse_out[0, :, 128 * p : 128 * p + 128] = (upper / lower).astype(BF)

    for wait in pending:
        wait()


def shards(
    image,
    timestep,
    class_label,
    class_table,
    fine_modulation,
    coarse_modulation,
    fine_project,
    fine_output,
    fine_scales,
    merge_weight,
    coarse_project,
    coarse_scales,
):
    hbm = pl.BlockSpec(memory_space=pl.ANY)
    vmem = pltpu.VMEM
    smem = pltpu.SMEM
    dma = pltpu.SemaphoreType.DMA
    return pl.pallas_call(
        kernel,
        out_shape=(
            pltpu.VMEM((4, 128, 256), BF),
            pltpu.VMEM((1, 32, 512), BF),
        ),
        in_specs=[hbm] * 12,
        out_specs=(pl.BlockSpec(memory_space=vmem),) * 2,
        scratch_shapes=[
            vmem((10, 128, 512), BF),
            vmem((1000, 256), BF),
            vmem((256, 512), BF),
            vmem((256, 512), BF),
            vmem((512, 768), BF),
            vmem((512, 768), BF),
            vmem((2, 2, 128, 512), BF),
            vmem((4, 2048, 512), BF),
            vmem((24, 512), BF),
            vmem((4, 4, 128, 256), BF),
            vmem((10, 128, 256), BF),
            vmem((10, 128, 256), BF),
            vmem((4, 128, 256), BF),
            vmem((4, 128, 256), BF),
            vmem((2, 16, 512), BF),
            vmem((8, 2, 16, 512), BF),
            vmem((2, 8, 512), F32),
            vmem((2, 4, 4, 32, 512), BF),
            vmem((2, 128, 128), BF),
            vmem((2, 128, 128), BF),
            vmem((2, 4, 2, 128, 128), BF),
            vmem((2, 2, 128, 128), BF),
            vmem((512, 128), F32),
            vmem((512, 128), F32),
            vmem((2, 8, 32, 128), BF),
            vmem((8, 2, 32, 128), BF),
            smem((1,), jnp.int32),
            smem((1,), jnp.int32),
            smem((8,), F32),
            smem((16,), F32),
            pltpu.SemaphoreType.REGULAR((3,)),
            dma((14,)),
            dma((4,)),
            dma((6,)),
            dma((6,)),
            dma((3,)),
            dma((3,)),
            dma((4,)),
            dma((4,)),
            dma((4,)),
            dma((8,)),
            dma((8,)),
            dma((16,)),
            dma((16,)),
            dma((8,)),
            dma((8,)),
            dma((4,)),
            dma((4,)),
            dma((4,)),
            dma((4,)),
            dma((16,)),
            dma((16,)),
        ],
        compiler_params=pltpu.CompilerParams(
            collective_id=0, has_side_effects=True, vmem_limit_bytes=56 * 1024 * 1024
        ),
    )(
        timestep,
        class_label,
        fine_scales,
        coarse_scales,
        image,
        class_table,
        fine_modulation,
        coarse_modulation,
        fine_project,
        fine_output.reshape(2, 128, 512),
        merge_weight.reshape(4, 2048, 512),
        coarse_project.T,
    )


def solution(mesh):
    in_specs = (
        P("band", None, None),
        P(),
        P(),
        P(),
        P(),
        P(None, "col"),
        P(None, "col"),
        P("col", None),
        P(),
        P(None, "col"),
        P("col", "band"),
        P(),
    )
    out_specs = (P("band", None, "col"), P("band", None, "col"))
    return jax.shard_map(shards, mesh=mesh, in_specs=in_specs, out_specs=out_specs, check_vma=False)
```

```python
import math

import jax
import jax.numpy as jnp
from jax import lax
from jax.experimental import pallas as pl
from jax.experimental.pallas import tpu as pltpu
from jax.sharding import PartitionSpec as P

EPSILON = 1e-06
LOG2E = math.log2(math.e)
BF = jnp.bfloat16
F32 = jnp.float32
MESH = pl.DeviceIdType.MESH
BANDS = 128
ORDER = (0, 1, 7, 2, 6, 3, 5, 4)


def dot(a, b):
    return jnp.dot(a, b, preferred_element_type=F32)


def dot_t(a, b):
    return lax.dot_general(a, b, (((1,), (1,)), ((), ())), preferred_element_type=F32)


def iota(shape, dim):
    return lax.broadcasted_iota(jnp.int32, shape, dim)


def kernel(
    timestep_h,
    label_h,
    fine_scales_h,
    coarse_scales_h,
    image,
    class_table,
    fine_modulation,
    coarse_modulation,
    fine_project,
    fine_output,
    merge_weight,
    coarse_project,
    fine_out,
    coarse_out,
    xb,
    table_v,
    fmod_v,
    cmod_v,
    fproj_v,
    wperm,
    fout_v,
    merge_v,
    cproj_v,
    qs,
    kb,
    vb,
    att_own,
    att_got,
    mg,
    gb,
    gain_v,
    wb,
    kvs,
    qsend,
    kvb,
    qb,
    num,
    ob,
    rb,
    timestep,
    label,
    fine_scales,
    coarse_scales,
    entered,
    load_sem,
    merge_sem,
    halo_send,
    halo_recv,
    pair_send,
    pair_recv,
    att_send,
    att_recv,
    fine_sem,
    w_send,
    w_recv,
    g_send,
    g_recv,
    kv_send,
    kv_recv,
    q_send,
    q_recv,
    fw_send,
    fw_recv,
    r_send,
    r_recv,
):
    band = lax.axis_index("band")
    c = lax.axis_index("col")
    core = lax.rem(band, 2)
    xh = lax.rem(lax.div(band, 2), 2)
    y = lax.rem(lax.div(band, 4), 4)
    z = lax.div(band, 16)
    x = 2 * xh + c

    def dev(zz, yy, xx, kk):
        return (((zz * 4 + yy) * 2 + lax.div(xx, 2)) * 2 + kk, lax.rem(xx, 2))

    sibling = dev(z, y, x, 1 - core)
    partner = (band, 1 - c)
    slow = (lax.rem(band + BANDS - 1 + 2 * core, BANDS), 1 - c)

    def row_of(u):
        return u + (1 - core) * (3 - 2 * u)

    def load(src, dst, k):
        return pltpu.make_async_copy(src, dst, load_sem.at[k])

    loads = [
        load(fine_modulation, fmod_v, 4),
        load(class_table, table_v, 5),
        load(fine_project, fproj_v, 6),
        load(coarse_modulation, cmod_v, 7),
        load(coarse_project, cproj_v, 8),
        load(fine_output, fout_v.at[c], 9),
    ]
    scalars = [
        load(timestep_h, timestep, 10),
        load(label_h, label, 11),
        load(fine_scales_h, fine_scales, 12),
        load(coarse_scales_h, coarse_scales, 13),
    ]
    for copy in scalars:
        copy.start()
    rows = [load(image.at[row_of(u)], xb.at[3 + u], u) for u in range(4)]
    merges = [
        pltpu.make_async_copy(merge_weight.at[row_of(u)], merge_v.at[u], merge_sem.at[u])
        for u in range(4)
    ]
    for copy in loads[:3]:
        copy.start()
    for copy in rows:
        copy.start()
    for copy in loads[3:]:
        copy.start()

    barrier = pltpu.get_barrier_semaphore()

    def signal(device):
        pl.semaphore_signal(barrier, inc=1, device_id=device, device_id_type=MESH)

    def near(dz, dy, dx):
        return dev(lax.rem(z + 8 + dz, 8), lax.rem(y + 4 + dy, 4), lax.rem(x + 4 + dx, 4), core)

    nearest = [near(*d) for d in ((0, 0, 1), (0, 0, -1), (0, 1, 0), (0, -1, 0), (1, 0, 0), (-1, 0, 0))]
    for device in [slow, sibling] + nearest:
        signal(device)

    pl.semaphore_wait(barrier, 8)

    def vouch(step, devices):
        for device in devices:
            pl.semaphore_signal(
                entered.at[step], inc=1, device_id=device, device_id_type=MESH
            )

    pending = []

    def loop(low, high, action):
        def step(k, carry):
            action(k)
            return carry

        lax.fori_loop(low, high, step, 0)

    def remote(src, dst, send, recv, device):
        return pltpu.make_async_remote_copy(
            src_ref=src,
            dst_ref=dst,
            send_sem=send,
            recv_sem=recv,
            device_id=device,
            device_id_type=MESH,
        )

    slow_copies = [
        remote(
            image.at[row_of(3 - j)], xb.at[7 + j], halo_send.at[j], halo_recv.at[j], slow
        )
        for j in range(3)
    ]
    fast_copies = [
        remote(
            image.at[row_of(j)], xb.at[2 - j], halo_send.at[3 + j], halo_recv.at[3 + j], sibling
        )
        for j in range(3)
    ]
    for copy in slow_copies + fast_copies:
        copy.start()
    pending.extend(copy.wait_send for copy in slow_copies + fast_copies)
    fout_copy = remote(
        fine_output.at[core], fout_v.at[c, core], pair_send.at[0], pair_recv.at[0], partner
    )
    fout_pass = remote(
        fout_v.at[1 - c, core],
        fout_v.at[1 - c, core],
        pair_send.at[2],
        pair_recv.at[2],
        sibling,
    )
    fout_copy.start()
    pending.append(fout_copy.wait_send)
    vouch(0, nearest)
    for copy in merges:
        copy.start()

    loads[4].wait()
    wb[core, y, x] = jnp.concatenate(
        [cproj_v[...].astype(F32), jnp.zeros((8, 512), F32)], axis=0
    ).astype(BF)

    def w_line(k):
        return remote(
            wb.at[core, y, x],
            wb.at[core, y, x],
            w_send.at[k],
            w_recv.at[k],
            dev(z, y, lax.rem(x + k, 4), core),
        )

    def w_plane(k):
        return remote(
            wb.at[core, y],
            wb.at[core, y],
            w_send.at[3 + k],
            w_recv.at[3 + k],
            dev(z, lax.rem(y + k, 4), x, core),
        )

    w_core = remote(wb.at[core], wb.at[core], w_send.at[0], w_recv.at[0], sibling)
    for copy in scalars:
        copy.wait()
    lane = iota((8, 256), 1)
    freq = jnp.exp((-math.log(10000.0) / 128.0) * lax.rem(lane, 128).astype(F32))
    angle = timestep[0].astype(F32) * freq
    time = jnp.where(lane < 128, jnp.cos(angle), jnp.sin(angle))
    one_hot = (iota((8, 1000), 1) == label[0]).astype(F32).astype(BF)
    loads[1].wait()
    condition = dot(one_hot, table_v[...]) + time
    c_hi = condition.astype(BF)
    rest = condition - c_hi.astype(F32)
    c_mid = rest.astype(BF)
    c_lo = (rest - c_mid.astype(F32)).astype(BF)

    def gain_of(weights):
        return 1.0 + (dot(c_hi, weights) + (dot(c_mid, weights) + dot(c_lo, weights)))

    loads[0].wait()
    fine_gain = gain_of(fmod_v[...])[0:1, :]
    loads[3].wait()
    gain_v[c] = gain_of(cmod_v[...])
    gain_copy = remote(gain_v.at[c], gain_v.at[c], pair_send.at[1], pair_recv.at[1], partner)
    gain_copy.start()
    pending.append(gain_copy.wait_send)

    loads[2].wait()
    fp = fproj_v[...]
    for part in range(3):
        for h in range(4):
            wperm[:, 256 * part + 64 * h : 256 * part + 64 * h + 64] = fp[
                :, 192 * h + 64 * part : 192 * h + 64 * part + 64
            ]
    ones_block = (lax.div(iota((256, 256), 0), 64) == lax.div(iota((256, 256), 1), 64)).astype(
        F32
    ).astype(BF)
    lane_head = lax.div(iota((1, 256), 1), 64)
    q_scale = jnp.zeros((1, 256), F32)
    for h in range(4):
        q_scale = jnp.where(lane_head == h, fine_scales[4 * c + h] * (LOG2E / 8.0), q_scale)

    def unit_factor(u):
        sq = u * u
        hi = sq.astype(BF)
        lo = (sq - hi.astype(F32)).astype(BF)
        return lax.rsqrt((dot(hi, ones_block) + dot(lo, ones_block)) * (1.0 / 64.0) + EPSILON)

    def normed_of(pixels):
        wide = pixels.astype(F32)
        mean = jnp.mean(wide * wide, axis=-1, keepdims=True)
        return (wide * lax.rsqrt(mean + EPSILON) * fine_gain).astype(BF)

    def keys_values(normed):
        kv = dot(normed, wperm[:, 256:768]).astype(BF)
        key = kv[:, :256].astype(F32)
        return (key * unit_factor(key) * 0.125).astype(BF), kv[:, 256:]

    for copy in rows:
        copy.wait()
    normed = normed_of(xb[3:7].reshape(512, 512))
    key, value = keys_values(normed)
    kb[3:7] = key.reshape(4, 128, 256)
    vb[3:7] = value.reshape(4, 128, 256)
    query = dot(normed, wperm[:, 0:256]).astype(BF).astype(F32)
    query = query * unit_factor(query) * q_scale
    for h in range(4):
        masked = jnp.where(lane_head == h, query, 0.0).astype(BF).reshape(4, 4, 32, 256)
        qs[:, :, 32 * h : 32 * h + 32, :] = masked
    for copy in fast_copies:
        copy.wait_recv()
    key, value = keys_values(normed_of(xb[0:3].reshape(384, 512)))
    kb[0:3] = key.reshape(3, 128, 256)
    vb[0:3] = value.reshape(3, 128, 256)

    first = (0, 16, 48, 64)
    column_gap = iota((32, 448), 0) - lax.rem(iota((32, 448), 1), 64)
    far = []
    for b in range(4):
        gap = column_gap + (32 * b - first[b])
        far.append(jnp.where((gap <= 3) & (gap >= -3), 0.0, -1e30))
    key_row = lax.div(iota((1, 448), 1), 64) - 3
    perm = (iota((128, 128), 1) == 4 * lax.rem(iota((128, 128), 0), 32) + lax.div(iota((128, 128), 0), 32)).astype(F32).astype(BF)

    def att_copy(r):
        return remote(att_own.at[r], att_got.at[r], att_send.at[r], att_recv.at[r], partner)

    def attend_row(r):
        slot = key_row + r
        row = 4 * band + slot + (1 - core) * (3 - 2 * slot)
        outside = jnp.where((row < 0) | (row >= 4 * BANDS), -1e30, 0.0)
        for b in range(4):
            keys = kb[pl.ds(r, 7), first[b] : first[b] + 64].reshape(448, 256)
            values = vb[pl.ds(r, 7), first[b] : first[b] + 64].reshape(448, 256)
            logits = dot_t(qs[r, b], keys).reshape(4, 32, 448) + (far[b] + outside)[None]
            weight = jnp.exp2(logits)
            total = jnp.sum(weight, axis=-1, keepdims=True)
            out = dot(weight.astype(BF).reshape(128, 448), values).reshape(4, 32, 256)
            out = out * (1.0 / total)
            mixed = jnp.zeros((32, 256), F32)
            for h in range(4):
                mixed = jnp.where(lane_head == h, out[h], mixed)
            att_own[r, 32 * b : 32 * b + 32] = mixed.astype(BF)
        att_copy(r).start()

    def mix_row(r):
        full = xb[3 + r].astype(F32) + dot(att_own[r], fout_v[c].reshape(256, 512))
        full = full + dot(att_got[r], fout_v[1 - c].reshape(256, 512))
        fine_out[row_of(r)] = jnp.where(c == 0, full[:, :256], full[:, 256:]).astype(BF)
        patches = dot(perm, full.astype(BF)).astype(BF)
        part = jnp.zeros((32, 512), F32)
        for p in range(4):
            part = part + dot(patches[32 * p : 32 * p + 32], merge_v[r, 512 * p : 512 * p + 512, :])
        return part

    def new_row(r):
        slow_copies[r - 1].wait_recv()
        key, value = keys_values(normed_of(xb[6 + r]))
        kb[6 + r] = key
        vb[6 + r] = value

    attend_row(0)
    pl.semaphore_wait(entered.at[0], 6)
    vouch(1, [near(2, 0, 0), near(-2, 0, 0), near(0, 2, 0)])
    for k in (2, 1, 3):
        w_line(k).start()
    loads[5].wait()
    fout_copy.wait_recv()
    fout_pass.start()
    pending.append(fout_pass.wait_send)
    new_row(1)
    attend_row(1)
    pl.semaphore_wait(entered.at[1], 3)
    vouch(2, [near(0, 0, 1), near(0, 0, -1), near(0, 0, 2)])
    new_row(2)
    attend_row(2)
    for k in (1, 2, 3):
        w_line(k).wait_recv()
    for k in (2, 1, 3):
        w_plane(k).start()
    new_row(3)
    attend_row(3)
    fout_pass.wait_recv()
    for copy in merges:
        copy.wait()
    for r in range(3):
        att_copy(r).wait_recv()
    merged = mix_row(0) + mix_row(1) + mix_row(2)
    att_copy(3).wait_recv()
    merged = (merged + mix_row(3)).astype(BF)
    pl.semaphore_wait(entered.at[2], 3)
    pending.extend(w_plane(k).wait_send for k in (1, 2, 3))

    def finish_row(r):
        att_copy(r).wait_send()

    pending.append(lambda: loop(0, 4, finish_row))

    mg[0] = merged[0:16]
    mg[1] = merged[16:32]
    gb[0, c] = mg[c]

    def g_copy(k):
        to_z = lax.rem(z + k // 2, 8)
        to_c = lax.rem(c + k % 2, 2)
        return remote(
            mg.at[to_c],
            gb.at[ORDER.index(k // 2), c],
            g_send.at[k],
            g_recv.at[k],
            dev(to_z, y, 2 * xh + to_c, core),
        )

    def g_wait(k):
        from_c = lax.rem(c + k % 2, 2)
        remote(
            mg.at[0],
            gb.at[ORDER.index(k // 2), from_c],
            g_send.at[k],
            g_recv.at[k],
            partner,
        ).wait_recv()

    sent = [2 * d + e for d in ORDER for e in range(2) if d + e > 0]
    for k in sent:
        g_copy(k).start()
    for k in (1, 2, 3):
        w_plane(k).wait_recv()
    for k in (1, 2, 3):
        w_line(k).wait_send()
    w_core.start()
    pending.append(w_core.wait_send)
    pending.extend(g_copy(k).wait_send for k in sent)

    prow = iota((256, 256), 0)
    plane_ = iota((256, 256), 1)
    inner = lax.rem(prow, 32)
    column = 24 * lax.div(prow, 32) + inner
    target = jnp.where(plane_ < 128, plane_ + 64, jnp.where(plane_ < 192, plane_ - 128, -1))
    select = ((inner < 24) & (column == target)).astype(F32).astype(BF)
    half = iota((64, 128), 1) < 64

    gain_copy.wait_recv()
    w_core.wait_recv()

    def project(part):
        for k in sent[:7] if part == 0 else sent[7:]:
            g_wait(k)
        x0 = gb[4 * part : 4 * part + 4, 0].reshape(64, 512).astype(F32)
        x1 = gb[4 * part : 4 * part + 4, 1].reshape(64, 512).astype(F32)
        square = jnp.sum(x0 * x0, axis=-1, keepdims=True) + jnp.sum(
            x1 * x1, axis=-1, keepdims=True
        )
        factor = lax.rsqrt(square * (1.0 / 1024.0) + EPSILON)
        s0 = (x0 * gain_v[0, 0:1, :]).astype(BF)
        s1 = (x1 * gain_v[1, 0:1, :]).astype(BF)
        for g in range(2):
            weights = [
                jnp.concatenate(
                    [wb[j % 2, 2 * g + j // 4, 2 * ((j // 2) % 2) + cc] for j in range(8)], axis=0
                )
                for cc in range(2)
            ]
            qkv = (dot_t(s0, weights[0]) + dot_t(s1, weights[1])) * factor
            qkv = dot(qkv.astype(BF), select)
            kv = qkv[:, :128]
            mean = jnp.sum(jnp.where(half, kv * kv, 0.0), axis=-1, keepdims=True) * (1.0 / 64.0)
            kvs[part, g] = jnp.where(half, kv * (lax.rsqrt(mean + EPSILON) * 0.125), kv).astype(BF)
            query = qkv[:, 128:]
            mean = jnp.sum(query * query, axis=-1, keepdims=True) * (1.0 / 64.0)
            scale = coarse_scales[2 * z + g] * (LOG2E / 8.0)
            qsend[g, 64 * part : 64 * part + 64] = (
                query * (lax.rsqrt(mean + EPSILON) * scale)
            ).astype(BF)

    def q_copy(k):
        to_xh = lax.rem(xh + lax.div(k, 2), 2)
        to_c = lax.rem(c + lax.rem(k, 2), 2)
        return remote(
            qsend.at[to_c],
            qb.at[xh, c],
            q_send.at[k],
            q_recv.at[k],
            dev(z, y, 2 * to_xh + to_c, core),
        )

    def kv_copy(part, k):
        to_y = lax.rem(y + k // 2, 4)
        to_c = lax.rem(c + k % 2, 2)
        return remote(
            kvs.at[part, to_c],
            kvb.at[part, core, y, c],
            kv_send.at[8 * part + k],
            kv_recv.at[8 * part + k],
            dev(z, to_y, 2 * xh + to_c, core),
        )

    def kv_wait(part, k):
        remote(
            kvs.at[part, 0],
            kvb.at[part, core, lax.rem(y + 4 - k // 2, 4), lax.rem(c + k % 2, 2)],
            kv_send.at[8 * part + k],
            kv_recv.at[8 * part + k],
            partner,
        ).wait_recv()

    def forward(part, k):
        from_y = lax.rem(y + 4 - k, 4)
        return remote(
            kvb.at[part, core, from_y],
            kvb.at[part, core, from_y],
            fw_send.at[4 * part + k],
            fw_recv.at[4 * part + k],
            sibling,
        )

    for part in range(2):
        project(part)
        for k in (4, 5, 2, 3, 6, 7, 1):
            kv_copy(part, k).start()
            pending.append(kv_copy(part, k).wait_send)
        kvb[part, core, y, c] = kvs[part, c]
    loop(1, 4, lambda k: q_copy(k).start())
    pending.append(lambda: loop(1, 4, lambda k: q_copy(k).wait_send()))
    qb[xh, c] = qsend[c]
    num[...] = jnp.zeros_like(num)
    half4 = iota((512, 128), 1) < 64

    def attend(part, which):
        block = kvb[part, which].reshape(512, 128)
        weight = jnp.exp2(dot_t(qb[...].reshape(512, 128), block)).astype(BF)
        num[...] += dot(weight, jnp.where(half4, 1.0, block.astype(F32)).astype(BF))

    def pass_on(part):
        for k in (1, 3, 2, 0):
            if k > 0:
                kv_wait(part, 2 * k)
            kv_wait(part, 2 * k + 1)
            forward(part, k).start()
            pending.append(forward(part, k).wait_send)

    pass_on(0)
    pass_on(1)
    loop(1, 4, lambda k: q_copy(k).wait_recv())
    attend(0, core)
    attend(1, core)
    for k in range(4):
        forward(0, k).wait_recv()
    attend(0, 1 - core)
    for k in range(4):
        forward(1, k).wait_recv()
    attend(1, 1 - core)
    result = num[...].astype(BF)
    for hi in range(2):
        for cc in range(2):
            for zz in range(8):
                start = ((hi * 2 + cc) * 8 + zz) * 16
                ob[hi, zz, 16 * cc : 16 * cc + 16] = result[start : start + 16]

    owner_c = lax.div(z, 4)

    def r_copy(k):
        to_z = lax.rem(z + k // 2, 8)
        to_xh = lax.rem(xh + k % 2, 2)
        slot = 2 * lax.rem(z, 4) + c
        return remote(
            ob.at[to_xh, ORDER.index((8 - k // 2) % 8)],
            rb.at[slot, xh],
            r_send.at[k],
            r_recv.at[2 * slot + xh],
            dev(to_z, y, 2 * to_xh + owner_c, core),
        )

    mine = owner_c == c

    @pl.when(jnp.logical_not(mine))
    def _():
        r_copy(0).start()

    for k in (8, 9, 7, 11, 6, 10, 5, 13, 4, 12, 3, 15, 2, 14, 1):
        r_copy(k).start()

    @pl.when(mine)
    def _():
        rb[2 * lax.rem(z, 4) + c, xh] = ob[xh, 0]

    own_slot = jnp.where(mine, 2 * (2 * lax.rem(z, 4) + c) + xh, -1)

    def r_wait(s):
        @pl.when(s != own_slot)
        def _():
            remote(
                ob.at[0, 0],
                rb.at[lax.div(s, 2), lax.rem(s, 2)],
                r_send.at[0],
                r_recv.at[s],
                partner,
            ).wait_recv()

    loop(0, 16, r_wait)

    def finish_returns():
        @pl.when(jnp.logical_not(mine))
        def _():
            r_copy(0).wait_send()

        for k in range(1, 16):
            r_copy(k).wait_send()

    pending.append(finish_returns)
    half3 = iota((32, 128), 1) < 64
    for p in range(4):
        even = rb[2 * p, 0].astype(F32) + rb[2 * p, 1].astype(F32)
        odd = rb[2 * p + 1, 0].astype(F32) + rb[2 * p + 1, 1].astype(F32)
        upper = jnp.where(half3, pltpu.roll(even, 64, 1), odd)
        lower = jnp.where(half3, even, pltpu.roll(odd, 64, 1))
        coarse_out[0, :, 128 * p : 128 * p + 128] = (upper / lower).astype(BF)

    for wait in pending:
        wait()


def shards(
    image,
    timestep,
    class_label,
    class_table,
    fine_modulation,
    coarse_modulation,
    fine_project,
    fine_output,
    fine_scales,
    merge_weight,
    coarse_project,
    coarse_scales,
):
    hbm = pl.BlockSpec(memory_space=pl.ANY)
    vmem = pltpu.VMEM
    smem = pltpu.SMEM
    dma = pltpu.SemaphoreType.DMA
    return pl.pallas_call(
        kernel,
        out_shape=(
            pltpu.VMEM((4, 128, 256), BF),
            pltpu.VMEM((1, 32, 512), BF),
        ),
        in_specs=[hbm] * 12,
        out_specs=(pl.BlockSpec(memory_space=vmem),) * 2,
        scratch_shapes=[
            vmem((10, 128, 512), BF),
            vmem((1000, 256), BF),
            vmem((256, 512), BF),
            vmem((256, 512), BF),
            vmem((512, 768), BF),
            vmem((512, 768), BF),
            vmem((2, 2, 128, 512), BF),
            vmem((4, 2048, 512), BF),
            vmem((24, 512), BF),
            vmem((4, 4, 128, 256), BF),
            vmem((10, 128, 256), BF),
            vmem((10, 128, 256), BF),
            vmem((4, 128, 256), BF),
            vmem((4, 128, 256), BF),
            vmem((2, 16, 512), BF),
            vmem((8, 2, 16, 512), BF),
            vmem((2, 8, 512), F32),
            vmem((2, 4, 4, 32, 512), BF),
            vmem((2, 2, 64, 128), BF),
            vmem((2, 128, 128), BF),
            vmem((2, 2, 4, 2, 64, 128), BF),
            vmem((2, 2, 128, 128), BF),
            vmem((512, 128), F32),
            vmem((2, 8, 32, 128), BF),
            vmem((8, 2, 32, 128), BF),
            smem((1,), jnp.int32),
            smem((1,), jnp.int32),
            smem((8,), F32),
            smem((16,), F32),
            pltpu.SemaphoreType.REGULAR((3,)),
            dma((14,)),
            dma((4,)),
            dma((6,)),
            dma((6,)),
            dma((3,)),
            dma((3,)),
            dma((4,)),
            dma((4,)),
            dma((4,)),
            dma((8,)),
            dma((8,)),
            dma((16,)),
            dma((16,)),
            dma((16,)),
            dma((16,)),
            dma((4,)),
            dma((4,)),
            dma((8,)),
            dma((8,)),
            dma((16,)),
            dma((16,)),
        ],
        compiler_params=pltpu.CompilerParams(
            collective_id=0, has_side_effects=True, vmem_limit_bytes=56 * 1024 * 1024
        ),
    )(
        timestep,
        class_label,
        fine_scales,
        coarse_scales,
        image,
        class_table,
        fine_modulation,
        coarse_modulation,
        fine_project,
        fine_output.reshape(2, 128, 512),
        merge_weight.reshape(4, 2048, 512),
        coarse_project.T,
    )


def solution(mesh):
    in_specs = (
        P("band", None, None),
        P(),
        P(),
        P(),
        P(),
        P(None, "col"),
        P(None, "col"),
        P("col", None),
        P(),
        P(None, "col"),
        P("col", "band"),
        P(),
    )
    out_specs = (P("band", None, "col"), P("band", None, "col"))
    return jax.shard_map(shards, mesh=mesh, in_specs=in_specs, out_specs=out_specs, check_vma=False)
```

```python
import math

import jax
import jax.numpy as jnp
from jax import lax
from jax.experimental import pallas as pl
from jax.experimental.pallas import tpu as pltpu
from jax.sharding import PartitionSpec as P

EPSILON = 1e-06
LOG2E = math.log2(math.e)
BF = jnp.bfloat16
F32 = jnp.float32
MESH = pl.DeviceIdType.MESH
BANDS = 128
ORDER = (0, 1, 7, 2, 6, 3, 5, 4)


def dot(a, b):
    return jnp.dot(a, b, preferred_element_type=F32)


def dot_t(a, b):
    return lax.dot_general(a, b, (((1,), (1,)), ((), ())), preferred_element_type=F32)


def iota(shape, dim):
    return lax.broadcasted_iota(jnp.int32, shape, dim)


def kernel(
    timestep_h,
    label_h,
    fine_scales_h,
    coarse_scales_h,
    image,
    class_table,
    fine_modulation,
    coarse_modulation,
    fine_project,
    fine_output,
    merge_weight,
    coarse_project,
    fine_out,
    coarse_out,
    xb,
    table_v,
    fmod_v,
    cmod_v,
    fproj_v,
    wperm,
    fout_v,
    merge_v,
    cproj_v,
    qs,
    kb,
    vb,
    att_own,
    att_got,
    mg,
    gb,
    gain_v,
    wb,
    wsel,
    kvs,
    qsend,
    kvb,
    qb,
    num,
    ob,
    rb,
    timestep,
    label,
    fine_scales,
    coarse_scales,
    entered,
    load_sem,
    merge_sem,
    halo_send,
    halo_recv,
    pair_send,
    pair_recv,
    att_send,
    att_recv,
    fine_sem,
    w_send,
    w_recv,
    g_send,
    g_recv,
    kv_send,
    kv_recv,
    q_send,
    q_recv,
    fw_send,
    fw_recv,
    r_send,
    r_recv,
):
    band = lax.axis_index("band")
    c = lax.axis_index("col")
    core = lax.rem(band, 2)
    xh = lax.rem(lax.div(band, 2), 2)
    y = lax.rem(lax.div(band, 4), 4)
    z = lax.div(band, 16)
    x = 2 * xh + c

    def dev(zz, yy, xx, kk):
        return (((zz * 4 + yy) * 2 + lax.div(xx, 2)) * 2 + kk, lax.rem(xx, 2))

    sibling = dev(z, y, x, 1 - core)
    partner = (band, 1 - c)
    slow = (lax.rem(band + BANDS - 1 + 2 * core, BANDS), 1 - c)

    def row_of(u):
        return u + (1 - core) * (3 - 2 * u)

    def load(src, dst, k):
        return pltpu.make_async_copy(src, dst, load_sem.at[k])

    loads = [
        load(fine_modulation, fmod_v, 4),
        load(class_table, table_v, 5),
        load(fine_project, fproj_v, 6),
        load(coarse_modulation, cmod_v, 7),
        load(coarse_project, cproj_v, 8),
        load(fine_output, fout_v.at[c], 9),
    ]
    scalars = [
        load(timestep_h, timestep, 10),
        load(label_h, label, 11),
        load(fine_scales_h, fine_scales, 12),
        load(coarse_scales_h, coarse_scales, 13),
    ]
    for copy in scalars:
        copy.start()
    rows = [load(image.at[row_of(u)], xb.at[3 + u], u) for u in range(4)]
    merges = [
        pltpu.make_async_copy(merge_weight.at[row_of(u)], merge_v.at[u], merge_sem.at[u])
        for u in range(4)
    ]
    for copy in loads[:3]:
        copy.start()
    for copy in rows:
        copy.start()
    for copy in loads[3:]:
        copy.start()

    barrier = pltpu.get_barrier_semaphore()

    def signal(device):
        pl.semaphore_signal(barrier, inc=1, device_id=device, device_id_type=MESH)

    def near(dz, dy, dx):
        return dev(lax.rem(z + 8 + dz, 8), lax.rem(y + 4 + dy, 4), lax.rem(x + 4 + dx, 4), core)

    nearest = [near(*d) for d in ((0, 0, 1), (0, 0, -1), (0, 1, 0), (0, -1, 0), (1, 0, 0), (-1, 0, 0))]
    for device in [slow, sibling] + nearest:
        signal(device)

    pl.semaphore_wait(barrier, 8)

    def vouch(step, devices):
        for device in devices:
            pl.semaphore_signal(
                entered.at[step], inc=1, device_id=device, device_id_type=MESH
            )

    pending = []

    def loop(low, high, action):
        def step(k, carry):
            action(k)
            return carry

        lax.fori_loop(low, high, step, 0)

    def remote(src, dst, send, recv, device):
        return pltpu.make_async_remote_copy(
            src_ref=src,
            dst_ref=dst,
            send_sem=send,
            recv_sem=recv,
            device_id=device,
            device_id_type=MESH,
        )

    slow_copies = [
        remote(
            image.at[row_of(3 - j)], xb.at[7 + j], halo_send.at[j], halo_recv.at[j], slow
        )
        for j in range(3)
    ]
    fast_copies = [
        remote(
            image.at[row_of(j)], xb.at[2 - j], halo_send.at[3 + j], halo_recv.at[3 + j], sibling
        )
        for j in range(3)
    ]
    for copy in slow_copies + fast_copies:
        copy.start()
    pending.extend(copy.wait_send for copy in slow_copies + fast_copies)
    fout_copy = remote(
        fine_output.at[core], fout_v.at[c, core], pair_send.at[0], pair_recv.at[0], partner
    )
    fout_pass = remote(
        fout_v.at[1 - c, core],
        fout_v.at[1 - c, core],
        pair_send.at[2],
        pair_recv.at[2],
        sibling,
    )
    fout_copy.start()
    pending.append(fout_copy.wait_send)
    vouch(0, nearest)
    for copy in merges:
        copy.start()

    loads[4].wait()
    wb[core, y, x] = jnp.concatenate(
        [cproj_v[...].astype(F32), jnp.zeros((8, 512), F32)], axis=0
    ).astype(BF)

    def w_line(k):
        return remote(
            wb.at[core, y, x],
            wb.at[core, y, x],
            w_send.at[k],
            w_recv.at[k],
            dev(z, y, lax.rem(x + k, 4), core),
        )

    def w_plane(k):
        return remote(
            wb.at[core, y],
            wb.at[core, y],
            w_send.at[3 + k],
            w_recv.at[3 + k],
            dev(z, lax.rem(y + k, 4), x, core),
        )

    w_core = remote(wb.at[core], wb.at[core], w_send.at[0], w_recv.at[0], sibling)
    for copy in scalars:
        copy.wait()
    lane = iota((8, 256), 1)
    freq = jnp.exp((-math.log(10000.0) / 128.0) * lax.rem(lane, 128).astype(F32))
    angle = timestep[0].astype(F32) * freq
    time = jnp.where(lane < 128, jnp.cos(angle), jnp.sin(angle))
    one_hot = (iota((8, 1000), 1) == label[0]).astype(F32).astype(BF)
    loads[1].wait()
    condition = dot(one_hot, table_v[...]) + time
    c_hi = condition.astype(BF)
    rest = condition - c_hi.astype(F32)
    c_mid = rest.astype(BF)
    c_lo = (rest - c_mid.astype(F32)).astype(BF)

    def gain_of(weights):
        return 1.0 + (dot(c_hi, weights) + (dot(c_mid, weights) + dot(c_lo, weights)))

    loads[0].wait()
    fine_gain = gain_of(fmod_v[...])[0:1, :]
    loads[3].wait()
    gain_v[c] = gain_of(cmod_v[...])
    gain_copy = remote(gain_v.at[c], gain_v.at[c], pair_send.at[1], pair_recv.at[1], partner)
    gain_copy.start()
    pending.append(gain_copy.wait_send)

    loads[2].wait()
    fp = fproj_v[...]
    for part in range(3):
        for h in range(4):
            wperm[:, 256 * part + 64 * h : 256 * part + 64 * h + 64] = fp[
                :, 192 * h + 64 * part : 192 * h + 64 * part + 64
            ]
    ones_block = (lax.div(iota((256, 256), 0), 64) == lax.div(iota((256, 256), 1), 64)).astype(
        F32
    ).astype(BF)
    lane_head = lax.div(iota((1, 256), 1), 64)
    q_scale = jnp.zeros((1, 256), F32)
    for h in range(4):
        q_scale = jnp.where(lane_head == h, fine_scales[4 * c + h] * (LOG2E / 8.0), q_scale)

    def unit_factor(u):
        sq = u * u
        hi = sq.astype(BF)
        lo = (sq - hi.astype(F32)).astype(BF)
        return lax.rsqrt((dot(hi, ones_block) + dot(lo, ones_block)) * (1.0 / 64.0) + EPSILON)

    def normed_of(pixels):
        wide = pixels.astype(F32)
        mean = jnp.mean(wide * wide, axis=-1, keepdims=True)
        return (wide * lax.rsqrt(mean + EPSILON) * fine_gain).astype(BF)

    def keys_values(normed):
        kv = dot(normed, wperm[:, 256:768]).astype(BF)
        key = kv[:, :256].astype(F32)
        return (key * unit_factor(key) * 0.125).astype(BF), kv[:, 256:]

    for copy in rows:
        copy.wait()
    normed = normed_of(xb[3:7].reshape(512, 512))
    key, value = keys_values(normed)
    kb[3:7] = key.reshape(4, 128, 256)
    vb[3:7] = value.reshape(4, 128, 256)
    query = dot(normed, wperm[:, 0:256]).astype(BF).astype(F32)
    query = query * unit_factor(query) * q_scale
    for h in range(4):
        masked = jnp.where(lane_head == h, query, 0.0).astype(BF).reshape(4, 4, 32, 256)
        qs[:, :, 32 * h : 32 * h + 32, :] = masked
    for copy in fast_copies:
        copy.wait_recv()
    key, value = keys_values(normed_of(xb[0:3].reshape(384, 512)))
    kb[0:3] = key.reshape(3, 128, 256)
    vb[0:3] = value.reshape(3, 128, 256)

    first = (0, 16, 48, 64)
    column_gap = iota((32, 448), 0) - lax.rem(iota((32, 448), 1), 64)
    far = []
    for b in range(4):
        gap = column_gap + (32 * b - first[b])
        far.append(jnp.where((gap <= 3) & (gap >= -3), 0.0, -1e30))
    key_row = lax.div(iota((1, 448), 1), 64) - 3
    perm = (iota((128, 128), 1) == 4 * lax.rem(iota((128, 128), 0), 32) + lax.div(iota((128, 128), 0), 32)).astype(F32).astype(BF)

    def att_copy(r):
        return remote(att_own.at[r], att_got.at[r], att_send.at[r], att_recv.at[r], partner)

    def attend_row(r):
        slot = key_row + r
        row = 4 * band + slot + (1 - core) * (3 - 2 * slot)
        outside = jnp.where((row < 0) | (row >= 4 * BANDS), -1e30, 0.0)
        for b in range(4):
            keys = kb[pl.ds(r, 7), first[b] : first[b] + 64].reshape(448, 256)
            values = vb[pl.ds(r, 7), first[b] : first[b] + 64].reshape(448, 256)
            logits = dot_t(qs[r, b], keys).reshape(4, 32, 448) + (far[b] + outside)[None]
            weight = jnp.exp2(logits)
            total = jnp.sum(weight, axis=-1, keepdims=True)
            out = dot(weight.astype(BF).reshape(128, 448), values).reshape(4, 32, 256)
            out = out * (1.0 / total)
            mixed = jnp.zeros((32, 256), F32)
            for h in range(4):
                mixed = jnp.where(lane_head == h, out[h], mixed)
            att_own[r, 32 * b : 32 * b + 32] = mixed.astype(BF)
        att_copy(r).start()

    def mix_row(r):
        full = xb[3 + r].astype(F32) + dot(att_own[r], fout_v[c].reshape(256, 512))
        full = full + dot(att_got[r], fout_v[1 - c].reshape(256, 512))
        fine_out[row_of(r)] = jnp.where(c == 0, full[:, :256], full[:, 256:]).astype(BF)
        patches = dot(perm, full.astype(BF)).astype(BF)
        part = jnp.zeros((32, 512), F32)
        for p in range(4):
            part = part + dot(patches[32 * p : 32 * p + 32], merge_v[r, 512 * p : 512 * p + 512, :])
        return part

    def new_row(r):
        slow_copies[r - 1].wait_recv()
        key, value = keys_values(normed_of(xb[6 + r]))
        kb[6 + r] = key
        vb[6 + r] = value

    attend_row(0)
    pl.semaphore_wait(entered.at[0], 6)
    vouch(1, [near(2, 0, 0), near(-2, 0, 0), near(0, 2, 0)])
    for k in (2, 1, 3):
        w_line(k).start()
    loads[5].wait()
    fout_copy.wait_recv()
    fout_pass.start()
    pending.append(fout_pass.wait_send)
    new_row(1)
    attend_row(1)
    pl.semaphore_wait(entered.at[1], 3)
    vouch(2, [near(0, 0, 1), near(0, 0, -1), near(0, 0, 2)])
    new_row(2)
    attend_row(2)
    for k in (1, 2, 3):
        w_line(k).wait_recv()
    for k in (2, 1, 3):
        w_plane(k).start()
    new_row(3)
    attend_row(3)
    fout_pass.wait_recv()
    for copy in merges:
        copy.wait()
    for r in range(3):
        att_copy(r).wait_recv()
    merged = mix_row(0) + mix_row(1) + mix_row(2)
    att_copy(3).wait_recv()
    merged = (merged + mix_row(3)).astype(BF)
    pl.semaphore_wait(entered.at[2], 3)
    pending.extend(w_plane(k).wait_send for k in (1, 2, 3))

    def finish_row(r):
        att_copy(r).wait_send()

    pending.append(lambda: loop(0, 4, finish_row))

    mg[0] = merged[0:16]
    mg[1] = merged[16:32]
    gb[0, c] = mg[c]

    def g_copy(k):
        to_z = lax.rem(z + k // 2, 8)
        to_c = lax.rem(c + k % 2, 2)
        return remote(
            mg.at[to_c],
            gb.at[ORDER.index(k // 2), c],
            g_send.at[k],
            g_recv.at[k],
            dev(to_z, y, 2 * xh + to_c, core),
        )

    def g_wait(k):
        from_c = lax.rem(c + k % 2, 2)
        remote(
            mg.at[0],
            gb.at[ORDER.index(k // 2), from_c],
            g_send.at[k],
            g_recv.at[k],
            partner,
        ).wait_recv()

    sent = [2 * d + e for d in ORDER for e in range(2) if d + e > 0]
    for k in sent:
        g_copy(k).start()
    for k in (1, 2, 3):
        w_plane(k).wait_recv()
    for k in (1, 2, 3):
        w_line(k).wait_send()
    w_core.start()
    pending.append(w_core.wait_send)
    pending.extend(g_copy(k).wait_send for k in sent)

    prow = iota((256, 256), 1)
    plane_ = iota((256, 256), 0)
    inner = lax.rem(prow, 32)
    column = 24 * lax.div(prow, 32) + inner
    target = jnp.where(plane_ < 128, plane_ + 64, jnp.where(plane_ < 192, plane_ - 128, -1))
    select = ((inner < 24) & (column == target)).astype(F32).astype(BF)
    half = iota((64, 128), 1) < 64

    gain_copy.wait_recv()
    w_core.wait_recv()
    for g in range(2):
        for cc in range(2):
            blocks = [wb[j % 2, 2 * g + j // 4, 2 * ((j // 2) % 2) + cc] for j in range(8)]
            wsel[g, cc] = dot(select, jnp.concatenate(blocks, axis=0)).astype(BF)

    def project(part):
        for k in sent[:7] if part == 0 else sent[7:]:
            g_wait(k)
        x0 = gb[4 * part : 4 * part + 4, 0].reshape(64, 512).astype(F32)
        x1 = gb[4 * part : 4 * part + 4, 1].reshape(64, 512).astype(F32)
        square = jnp.sum(x0 * x0, axis=-1, keepdims=True) + jnp.sum(
            x1 * x1, axis=-1, keepdims=True
        )
        factor = lax.rsqrt(square * (1.0 / 1024.0) + EPSILON)
        s0 = (x0 * gain_v[0, 0:1, :]).astype(BF)
        s1 = (x1 * gain_v[1, 0:1, :]).astype(BF)
        for g in range(2):
            qkv = (dot_t(s0, wsel[g, 0]) + dot_t(s1, wsel[g, 1])) * factor
            qkv = qkv.astype(BF).astype(F32)
            kv = qkv[:, :128]
            mean = jnp.sum(jnp.where(half, kv * kv, 0.0), axis=-1, keepdims=True) * (1.0 / 64.0)
            kvs[part, g] = jnp.where(half, kv * (lax.rsqrt(mean + EPSILON) * 0.125), kv).astype(BF)
            query = qkv[:, 128:]
            mean = jnp.sum(query * query, axis=-1, keepdims=True) * (1.0 / 64.0)
            scale = coarse_scales[2 * z + g] * (LOG2E / 8.0)
            qsend[g, 64 * part : 64 * part + 64] = (
                query * (lax.rsqrt(mean + EPSILON) * scale)
            ).astype(BF)

    def q_copy(k):
        to_xh = lax.rem(xh + lax.div(k, 2), 2)
        to_c = lax.rem(c + lax.rem(k, 2), 2)
        return remote(
            qsend.at[to_c],
            qb.at[xh, c],
            q_send.at[k],
            q_recv.at[k],
            dev(z, y, 2 * to_xh + to_c, core),
        )

    def kv_copy(part, k):
        to_y = lax.rem(y + k // 2, 4)
        to_c = lax.rem(c + k % 2, 2)
        return remote(
            kvs.at[part, to_c],
            kvb.at[part, core, y, c],
            kv_send.at[8 * part + k],
            kv_recv.at[8 * part + k],
            dev(z, to_y, 2 * xh + to_c, core),
        )

    def kv_wait(part, k):
        remote(
            kvs.at[part, 0],
            kvb.at[part, core, lax.rem(y + 4 - k // 2, 4), lax.rem(c + k % 2, 2)],
            kv_send.at[8 * part + k],
            kv_recv.at[8 * part + k],
            partner,
        ).wait_recv()

    def forward(part, k):
        from_y = lax.rem(y + 4 - k, 4)
        return remote(
            kvb.at[part, core, from_y],
            kvb.at[part, core, from_y],
            fw_send.at[4 * part + k],
            fw_recv.at[4 * part + k],
            sibling,
        )

    for part in range(2):
        project(part)
        for k in (4, 5, 2, 3, 6, 7, 1):
            kv_copy(part, k).start()
            pending.append(kv_copy(part, k).wait_send)
        kvb[part, core, y, c] = kvs[part, c]
    loop(1, 4, lambda k: q_copy(k).start())
    pending.append(lambda: loop(1, 4, lambda k: q_copy(k).wait_send()))
    qb[xh, c] = qsend[c]
    num[...] = jnp.zeros_like(num)
    half4 = iota((512, 128), 1) < 64

    def attend(part, which):
        block = kvb[part, which].reshape(512, 128)
        weight = jnp.exp2(dot_t(qb[...].reshape(512, 128), block)).astype(BF)
        num[...] += dot(weight, jnp.where(half4, 1.0, block.astype(F32)).astype(BF))

    def pass_on(part):
        for k in (1, 3, 2, 0):
            if k > 0:
                kv_wait(part, 2 * k)
            kv_wait(part, 2 * k + 1)
            forward(part, k).start()
            pending.append(forward(part, k).wait_send)

    pass_on(0)
    pass_on(1)
    loop(1, 4, lambda k: q_copy(k).wait_recv())
    attend(0, core)
    attend(1, core)
    for k in range(4):
        forward(0, k).wait_recv()
    attend(0, 1 - core)
    for k in range(4):
        forward(1, k).wait_recv()
    attend(1, 1 - core)
    result = num[...].astype(BF)
    for hi in range(2):
        for cc in range(2):
            for zz in range(8):
                start = ((hi * 2 + cc) * 8 + zz) * 16
                ob[hi, zz, 16 * cc : 16 * cc + 16] = result[start : start + 16]

    owner_c = lax.div(z, 4)

    def r_copy(k):
        to_z = lax.rem(z + k // 2, 8)
        to_xh = lax.rem(xh + k % 2, 2)
        slot = 2 * lax.rem(z, 4) + c
        return remote(
            ob.at[to_xh, ORDER.index((8 - k // 2) % 8)],
            rb.at[slot, xh],
            r_send.at[k],
            r_recv.at[2 * slot + xh],
            dev(to_z, y, 2 * to_xh + owner_c, core),
        )

    mine = owner_c == c

    @pl.when(jnp.logical_not(mine))
    def _():
        r_copy(0).start()

    for k in (8, 9, 7, 11, 6, 10, 5, 13, 4, 12, 3, 15, 2, 14, 1):
        r_copy(k).start()

    @pl.when(mine)
    def _():
        rb[2 * lax.rem(z, 4) + c, xh] = ob[xh, 0]

    own_slot = jnp.where(mine, 2 * (2 * lax.rem(z, 4) + c) + xh, -1)

    def r_wait(s):
        @pl.when(s != own_slot)
        def _():
            remote(
                ob.at[0, 0],
                rb.at[lax.div(s, 2), lax.rem(s, 2)],
                r_send.at[0],
                r_recv.at[s],
                partner,
            ).wait_recv()


    def finish_returns():
        @pl.when(jnp.logical_not(mine))
        def _():
            r_copy(0).wait_send()

        for k in range(1, 16):
            r_copy(k).wait_send()

    pending.append(finish_returns)
    for wait in pending:
        wait()
    loop(0, 16, r_wait)
    half3 = iota((32, 128), 1) < 64
    for p in range(4):
        even = rb[2 * p, 0].astype(F32) + rb[2 * p, 1].astype(F32)
        odd = rb[2 * p + 1, 0].astype(F32) + rb[2 * p + 1, 1].astype(F32)
        upper = jnp.where(half3, pltpu.roll(even, 64, 1), odd)
        lower = jnp.where(half3, even, pltpu.roll(odd, 64, 1))
        coarse_out[0, :, 128 * p : 128 * p + 128] = (upper / lower).astype(BF)


def shards(
    image,
    timestep,
    class_label,
    class_table,
    fine_modulation,
    coarse_modulation,
    fine_project,
    fine_output,
    fine_scales,
    merge_weight,
    coarse_project,
    coarse_scales,
):
    hbm = pl.BlockSpec(memory_space=pl.ANY)
    vmem = pltpu.VMEM
    smem = pltpu.SMEM
    dma = pltpu.SemaphoreType.DMA
    return pl.pallas_call(
        kernel,
        out_shape=(
            pltpu.VMEM((4, 128, 256), BF),
            pltpu.VMEM((1, 32, 512), BF),
        ),
        in_specs=[hbm] * 12,
        out_specs=(pl.BlockSpec(memory_space=vmem),) * 2,
        scratch_shapes=[
            vmem((10, 128, 512), BF),
            vmem((1000, 256), BF),
            vmem((256, 512), BF),
            vmem((256, 512), BF),
            vmem((512, 768), BF),
            vmem((512, 768), BF),
            vmem((2, 2, 128, 512), BF),
            vmem((4, 2048, 512), BF),
            vmem((24, 512), BF),
            vmem((4, 4, 128, 256), BF),
            vmem((10, 128, 256), BF),
            vmem((10, 128, 256), BF),
            vmem((4, 128, 256), BF),
            vmem((4, 128, 256), BF),
            vmem((2, 16, 512), BF),
            vmem((8, 2, 16, 512), BF),
            vmem((2, 8, 512), F32),
            vmem((2, 4, 4, 32, 512), BF),
            vmem((2, 2, 256, 512), BF),
            vmem((2, 2, 64, 128), BF),
            vmem((2, 128, 128), BF),
            vmem((2, 2, 4, 2, 64, 128), BF),
            vmem((2, 2, 128, 128), BF),
            vmem((512, 128), F32),
            vmem((2, 8, 32, 128), BF),
            vmem((8, 2, 32, 128), BF),
            smem((1,), jnp.int32),
            smem((1,), jnp.int32),
            smem((8,), F32),
            smem((16,), F32),
            pltpu.SemaphoreType.REGULAR((3,)),
            dma((14,)),
            dma((4,)),
            dma((6,)),
            dma((6,)),
            dma((3,)),
            dma((3,)),
            dma((4,)),
            dma((4,)),
            dma((4,)),
            dma((8,)),
            dma((8,)),
            dma((16,)),
            dma((16,)),
            dma((16,)),
            dma((16,)),
            dma((4,)),
            dma((4,)),
            dma((8,)),
            dma((8,)),
            dma((16,)),
            dma((16,)),
        ],
        compiler_params=pltpu.CompilerParams(
            collective_id=0, has_side_effects=True, vmem_limit_bytes=56 * 1024 * 1024
        ),
    )(
        timestep,
        class_label,
        fine_scales,
        coarse_scales,
        image,
        class_table,
        fine_modulation,
        coarse_modulation,
        fine_project,
        fine_output.reshape(2, 128, 512),
        merge_weight.reshape(4, 2048, 512),
        coarse_project.T,
    )


def solution(mesh):
    in_specs = (
        P("band", None, None),
        P(),
        P(),
        P(),
        P(),
        P(None, "col"),
        P(None, "col"),
        P("col", None),
        P(),
        P(None, "col"),
        P("col", "band"),
        P(),
    )
    out_specs = (P("band", None, "col"), P("band", None, "col"))
    return jax.shard_map(shards, mesh=mesh, in_specs=in_specs, out_specs=out_specs, check_vma=False)
```

```python
import math

import jax
import jax.numpy as jnp
from jax import lax
from jax.experimental import pallas as pl
from jax.experimental.pallas import tpu as pltpu
from jax.sharding import PartitionSpec as P

EPSILON = 1e-06
LOG2E = math.log2(math.e)
BF = jnp.bfloat16
F32 = jnp.float32
MESH = pl.DeviceIdType.MESH
BANDS = 128
ORDER = (0, 1, 7, 2, 6, 3, 5, 4)


def dot(a, b):
    return jnp.dot(a, b, preferred_element_type=F32)


def dot_t(a, b):
    return lax.dot_general(a, b, (((1,), (1,)), ((), ())), preferred_element_type=F32)


def iota(shape, dim):
    return lax.broadcasted_iota(jnp.int32, shape, dim)


def kernel(
    timestep_h,
    label_h,
    fine_scales_h,
    coarse_scales_h,
    image,
    class_table,
    fine_modulation,
    coarse_modulation,
    fine_project,
    fine_output,
    merge_weight,
    coarse_project,
    fine_out,
    coarse_out,
    xb,
    table_v,
    fmod_v,
    cmod_v,
    fproj_v,
    wperm,
    fout_v,
    merge_v,
    cproj_v,
    qs,
    kb,
    vb,
    att_own,
    att_got,
    mg,
    gb,
    gain_v,
    wb,
    wsel,
    kvs,
    qsend,
    kvb,
    qb,
    num,
    ob,
    rb,
    timestep,
    label,
    fine_scales,
    coarse_scales,
    entered,
    load_sem,
    merge_sem,
    halo_send,
    halo_recv,
    pair_send,
    pair_recv,
    att_send,
    att_recv,
    fine_sem,
    w_send,
    w_recv,
    g_send,
    g_recv,
    kv_send,
    kv_recv,
    q_send,
    q_recv,
    fw_send,
    fw_recv,
    r_send,
    r_recv,
):
    band = lax.axis_index("band")
    c = lax.axis_index("col")
    core = lax.rem(band, 2)
    xh = lax.rem(lax.div(band, 2), 2)
    y = lax.rem(lax.div(band, 4), 4)
    z = lax.div(band, 16)
    x = 2 * xh + c

    def dev(zz, yy, xx, kk):
        return (((zz * 4 + yy) * 2 + lax.div(xx, 2)) * 2 + kk, lax.rem(xx, 2))

    sibling = dev(z, y, x, 1 - core)
    partner = (band, 1 - c)
    slow = (lax.rem(band + BANDS - 1 + 2 * core, BANDS), 1 - c)

    def row_of(u):
        return u + (1 - core) * (3 - 2 * u)

    def load(src, dst, k):
        return pltpu.make_async_copy(src, dst, load_sem.at[k])

    loads = [
        load(fine_modulation, fmod_v, 4),
        load(class_table, table_v, 5),
        load(fine_project, fproj_v, 6),
        load(coarse_modulation, cmod_v, 7),
        load(coarse_project, cproj_v, 8),
        load(fine_output, fout_v.at[c], 9),
    ]
    scalars = [
        load(timestep_h, timestep, 10),
        load(label_h, label, 11),
        load(fine_scales_h, fine_scales, 12),
        load(coarse_scales_h, coarse_scales, 13),
    ]
    for copy in scalars:
        copy.start()
    rows = [load(image.at[row_of(u)], xb.at[3 + u], u) for u in range(4)]
    merges = [
        pltpu.make_async_copy(merge_weight.at[row_of(u)], merge_v.at[u], merge_sem.at[u])
        for u in range(4)
    ]
    for copy in loads[:3]:
        copy.start()
    for copy in rows:
        copy.start()
    for copy in loads[3:]:
        copy.start()

    barrier = pltpu.get_barrier_semaphore()

    def signal(device):
        pl.semaphore_signal(barrier, inc=1, device_id=device, device_id_type=MESH)

    def near(dz, dy, dx):
        return dev(lax.rem(z + 8 + dz, 8), lax.rem(y + 4 + dy, 4), lax.rem(x + 4 + dx, 4), core)

    nearest = [near(*d) for d in ((0, 0, 1), (0, 0, -1), (0, 1, 0), (0, -1, 0), (1, 0, 0), (-1, 0, 0))]
    for device in [slow, sibling] + nearest:
        signal(device)

    pl.semaphore_wait(barrier, 8)

    def vouch(step, devices):
        for device in devices:
            pl.semaphore_signal(
                entered.at[step], inc=1, device_id=device, device_id_type=MESH
            )

    pending = []

    def loop(low, high, action):
        def step(k, carry):
            action(k)
            return carry

        lax.fori_loop(low, high, step, 0)

    def remote(src, dst, send, recv, device):
        return pltpu.make_async_remote_copy(
            src_ref=src,
            dst_ref=dst,
            send_sem=send,
            recv_sem=recv,
            device_id=device,
            device_id_type=MESH,
        )

    slow_copies = [
        remote(
            image.at[row_of(3 - j)], xb.at[7 + j], halo_send.at[j], halo_recv.at[j], slow
        )
        for j in range(3)
    ]
    fast_copies = [
        remote(
            image.at[row_of(j)], xb.at[2 - j], halo_send.at[3 + j], halo_recv.at[3 + j], sibling
        )
        for j in range(3)
    ]
    for copy in slow_copies + fast_copies:
        copy.start()
    pending.extend(copy.wait_send for copy in slow_copies + fast_copies)
    fout_copy = remote(
        fine_output.at[core], fout_v.at[c, core], pair_send.at[0], pair_recv.at[0], partner
    )
    fout_pass = remote(
        fout_v.at[1 - c, core],
        fout_v.at[1 - c, core],
        pair_send.at[2],
        pair_recv.at[2],
        sibling,
    )
    fout_copy.start()
    pending.append(fout_copy.wait_send)
    vouch(0, nearest)
    for copy in merges:
        copy.start()

    loads[4].wait()
    wb[core, y, x] = jnp.concatenate(
        [cproj_v[...].astype(F32), jnp.zeros((8, 512), F32)], axis=0
    ).astype(BF)

    def w_line(k):
        return remote(
            wb.at[core, y, x],
            wb.at[core, y, x],
            w_send.at[k],
            w_recv.at[k],
            dev(z, y, lax.rem(x + k, 4), core),
        )

    def w_plane(k):
        return remote(
            wb.at[core, y],
            wb.at[core, y],
            w_send.at[3 + k],
            w_recv.at[3 + k],
            dev(z, lax.rem(y + k, 4), x, core),
        )

    w_core = remote(wb.at[core], wb.at[core], w_send.at[0], w_recv.at[0], sibling)
    for copy in scalars:
        copy.wait()
    lane = iota((8, 256), 1)
    freq = jnp.exp((-math.log(10000.0) / 128.0) * lax.rem(lane, 128).astype(F32))
    angle = timestep[0].astype(F32) * freq
    time = jnp.where(lane < 128, jnp.cos(angle), jnp.sin(angle))
    one_hot = (iota((8, 1000), 1) == label[0]).astype(F32).astype(BF)
    loads[1].wait()
    condition = dot(one_hot, table_v[...]) + time
    c_hi = condition.astype(BF)
    rest = condition - c_hi.astype(F32)
    c_mid = rest.astype(BF)
    c_lo = (rest - c_mid.astype(F32)).astype(BF)

    def gain_of(weights):
        return 1.0 + (dot(c_hi, weights) + (dot(c_mid, weights) + dot(c_lo, weights)))

    loads[0].wait()
    fine_gain = gain_of(fmod_v[...])[0:1, :]
    loads[3].wait()
    gain_v[c] = gain_of(cmod_v[...])
    gain_copy = remote(gain_v.at[c], gain_v.at[c], pair_send.at[1], pair_recv.at[1], partner)
    gain_copy.start()
    pending.append(gain_copy.wait_send)

    loads[2].wait()
    fp = fproj_v[...]
    for part in range(3):
        for h in range(4):
            wperm[:, 256 * part + 64 * h : 256 * part + 64 * h + 64] = fp[
                :, 192 * h + 64 * part : 192 * h + 64 * part + 64
            ]
    ones_block = (lax.div(iota((256, 256), 0), 64) == lax.div(iota((256, 256), 1), 64)).astype(
        F32
    ).astype(BF)
    lane_head = lax.div(iota((1, 256), 1), 64)
    q_scale = jnp.zeros((1, 256), F32)
    for h in range(4):
        q_scale = jnp.where(lane_head == h, fine_scales[4 * c + h] * (LOG2E / 8.0), q_scale)

    def unit_factor(u):
        sq = u * u
        hi = sq.astype(BF)
        lo = (sq - hi.astype(F32)).astype(BF)
        return lax.rsqrt((dot(hi, ones_block) + dot(lo, ones_block)) * (1.0 / 64.0) + EPSILON)

    def normed_of(pixels):
        wide = pixels.astype(F32)
        mean = jnp.mean(wide * wide, axis=-1, keepdims=True)
        return (wide * lax.rsqrt(mean + EPSILON) * fine_gain).astype(BF)

    def keys_values(normed):
        kv = dot(normed, wperm[:, 256:768]).astype(BF)
        key = kv[:, :256].astype(F32)
        return (key * unit_factor(key) * 0.125).astype(BF), kv[:, 256:]

    for copy in rows:
        copy.wait()
    normed = normed_of(xb[3:7].reshape(512, 512))
    key, value = keys_values(normed)
    kb[3:7] = key.reshape(4, 128, 256)
    vb[3:7] = value.reshape(4, 128, 256)
    query = dot(normed, wperm[:, 0:256]).astype(BF).astype(F32)
    query = query * unit_factor(query) * q_scale
    for h in range(4):
        masked = jnp.where(lane_head == h, query, 0.0).astype(BF).reshape(4, 4, 32, 256)
        qs[:, :, 32 * h : 32 * h + 32, :] = masked
    for copy in fast_copies:
        copy.wait_recv()
    key, value = keys_values(normed_of(xb[0:3].reshape(384, 512)))
    kb[0:3] = key.reshape(3, 128, 256)
    vb[0:3] = value.reshape(3, 128, 256)

    first = (0, 16, 48, 64)
    column_gap = iota((32, 448), 0) - lax.rem(iota((32, 448), 1), 64)
    far = []
    for b in range(4):
        gap = column_gap + (32 * b - first[b])
        far.append(jnp.where((gap <= 3) & (gap >= -3), 0.0, -1e30))
    key_row = lax.div(iota((1, 448), 1), 64) - 3
    perm = (iota((128, 128), 1) == 4 * lax.rem(iota((128, 128), 0), 32) + lax.div(iota((128, 128), 0), 32)).astype(F32).astype(BF)

    def att_copy(r):
        return remote(att_own.at[r], att_got.at[r], att_send.at[r], att_recv.at[r], partner)

    def attend_row(r):
        slot = key_row + r
        row = 4 * band + slot + (1 - core) * (3 - 2 * slot)
        outside = jnp.where((row < 0) | (row >= 4 * BANDS), -1e30, 0.0)
        for b in range(4):
            keys = kb[pl.ds(r, 7), first[b] : first[b] + 64].reshape(448, 256)
            values = vb[pl.ds(r, 7), first[b] : first[b] + 64].reshape(448, 256)
            logits = dot_t(qs[r, b], keys).reshape(4, 32, 448) + (far[b] + outside)[None]
            weight = jnp.exp2(logits)
            total = jnp.sum(weight, axis=-1, keepdims=True)
            out = dot(weight.astype(BF).reshape(128, 448), values).reshape(4, 32, 256)
            out = out * (1.0 / total)
            mixed = jnp.zeros((32, 256), F32)
            for h in range(4):
                mixed = jnp.where(lane_head == h, out[h], mixed)
            att_own[r, 32 * b : 32 * b + 32] = mixed.astype(BF)
        att_copy(r).start()

    def mix_row(r):
        full = xb[3 + r].astype(F32) + dot(att_own[r], fout_v[c].reshape(256, 512))
        full = full + dot(att_got[r], fout_v[1 - c].reshape(256, 512))
        fine_out[row_of(r)] = jnp.where(c == 0, full[:, :256], full[:, 256:]).astype(BF)
        patches = dot(perm, full.astype(BF)).astype(BF)
        part = jnp.zeros((32, 512), F32)
        for p in range(4):
            part = part + dot(patches[32 * p : 32 * p + 32], merge_v[r, 512 * p : 512 * p + 512, :])
        return part

    def new_row(r):
        slow_copies[r - 1].wait_recv()
        key, value = keys_values(normed_of(xb[6 + r]))
        kb[6 + r] = key
        vb[6 + r] = value

    attend_row(0)
    pl.semaphore_wait(entered.at[0], 6)
    vouch(1, [near(2, 0, 0), near(-2, 0, 0), near(0, 2, 0)])
    for k in (2, 1, 3):
        w_line(k).start()
    loads[5].wait()
    fout_copy.wait_recv()
    fout_pass.start()
    pending.append(fout_pass.wait_send)
    new_row(1)
    attend_row(1)
    pl.semaphore_wait(entered.at[1], 3)
    vouch(2, [near(0, 0, 1), near(0, 0, -1), near(0, 0, 2)])
    new_row(2)
    attend_row(2)
    for k in (1, 2, 3):
        w_line(k).wait_recv()
    for k in (2, 1, 3):
        w_plane(k).start()
    fout_pass.wait_recv()
    merges[0].wait()
    att_copy(0).wait_recv()
    merged = mix_row(0)
    new_row(3)
    attend_row(3)
    for r in (1, 2):
        merges[r].wait()
        att_copy(r).wait_recv()
    merges[3].wait()
    merged = merged + (mix_row(1) + mix_row(2))
    att_copy(3).wait_recv()
    merged = (merged + mix_row(3)).astype(BF)
    pl.semaphore_wait(entered.at[2], 3)
    pending.extend(w_plane(k).wait_send for k in (1, 2, 3))

    def finish_row(r):
        att_copy(r).wait_send()

    pending.append(lambda: loop(0, 4, finish_row))

    mg[0] = merged[0:16]
    mg[1] = merged[16:32]
    gb[0, c] = mg[c]

    def g_copy(k):
        to_z = lax.rem(z + k // 2, 8)
        to_c = lax.rem(c + k % 2, 2)
        return remote(
            mg.at[to_c],
            gb.at[ORDER.index(k // 2), c],
            g_send.at[k],
            g_recv.at[k],
            dev(to_z, y, 2 * xh + to_c, core),
        )

    def g_wait(k):
        from_c = lax.rem(c + k % 2, 2)
        remote(
            mg.at[0],
            gb.at[ORDER.index(k // 2), from_c],
            g_send.at[k],
            g_recv.at[k],
            partner,
        ).wait_recv()

    sent = [2 * d + e for d in ORDER for e in range(2) if d + e > 0]
    for k in sent:
        g_copy(k).start()
    for k in (1, 2, 3):
        w_plane(k).wait_recv()
    for k in (1, 2, 3):
        w_line(k).wait_send()
    w_core.start()
    pending.append(w_core.wait_send)
    pending.extend(g_copy(k).wait_send for k in sent)

    prow = iota((256, 256), 1)
    plane_ = iota((256, 256), 0)
    inner = lax.rem(prow, 32)
    column = 24 * lax.div(prow, 32) + inner
    target = jnp.where(plane_ < 128, plane_ + 64, jnp.where(plane_ < 192, plane_ - 128, -1))
    select = ((inner < 24) & (column == target)).astype(F32).astype(BF)
    half = iota((64, 128), 1) < 64

    gain_copy.wait_recv()
    w_core.wait_recv()
    for g in range(2):
        for cc in range(2):
            blocks = [wb[j % 2, 2 * g + j // 4, 2 * ((j // 2) % 2) + cc] for j in range(8)]
            wsel[g, cc] = dot(select, jnp.concatenate(blocks, axis=0)).astype(BF)

    def project(part):
        for k in sent[:7] if part == 0 else sent[7:]:
            g_wait(k)
        x0 = gb[4 * part : 4 * part + 4, 0].reshape(64, 512).astype(F32)
        x1 = gb[4 * part : 4 * part + 4, 1].reshape(64, 512).astype(F32)
        square = jnp.sum(x0 * x0, axis=-1, keepdims=True) + jnp.sum(
            x1 * x1, axis=-1, keepdims=True
        )
        factor = lax.rsqrt(square * (1.0 / 1024.0) + EPSILON)
        s0 = (x0 * gain_v[0, 0:1, :]).astype(BF)
        s1 = (x1 * gain_v[1, 0:1, :]).astype(BF)
        for g in range(2):
            qkv = (dot_t(s0, wsel[g, 0]) + dot_t(s1, wsel[g, 1])) * factor
            qkv = qkv.astype(BF).astype(F32)
            kv = qkv[:, :128]
            mean = jnp.sum(jnp.where(half, kv * kv, 0.0), axis=-1, keepdims=True) * (1.0 / 64.0)
            kvs[part, g] = jnp.where(half, kv * (lax.rsqrt(mean + EPSILON) * 0.125), kv).astype(BF)
            query = qkv[:, 128:]
            mean = jnp.sum(query * query, axis=-1, keepdims=True) * (1.0 / 64.0)
            scale = coarse_scales[2 * z + g] * (LOG2E / 8.0)
            qsend[g, 64 * part : 64 * part + 64] = (
                query * (lax.rsqrt(mean + EPSILON) * scale)
            ).astype(BF)

    def q_copy(k):
        to_xh = lax.rem(xh + lax.div(k, 2), 2)
        to_c = lax.rem(c + lax.rem(k, 2), 2)
        return remote(
            qsend.at[to_c],
            qb.at[xh, c],
            q_send.at[k],
            q_recv.at[k],
            dev(z, y, 2 * to_xh + to_c, core),
        )

    def kv_copy(part, k):
        to_y = lax.rem(y + k // 2, 4)
        to_c = lax.rem(c + k % 2, 2)
        return remote(
            kvs.at[part, to_c],
            kvb.at[part, core, y, c],
            kv_send.at[8 * part + k],
            kv_recv.at[8 * part + k],
            dev(z, to_y, 2 * xh + to_c, core),
        )

    def kv_wait(part, k):
        remote(
            kvs.at[part, 0],
            kvb.at[part, core, lax.rem(y + 4 - k // 2, 4), lax.rem(c + k % 2, 2)],
            kv_send.at[8 * part + k],
            kv_recv.at[8 * part + k],
            partner,
        ).wait_recv()

    def forward(part, k):
        from_y = lax.rem(y + 4 - k, 4)
        return remote(
            kvb.at[part, core, from_y],
            kvb.at[part, core, from_y],
            fw_send.at[4 * part + k],
            fw_recv.at[4 * part + k],
            sibling,
        )

    for part in range(2):
        project(part)
        for k in (4, 5, 2, 3, 6, 7, 1):
            kv_copy(part, k).start()
            pending.append(kv_copy(part, k).wait_send)
        kvb[part, core, y, c] = kvs[part, c]
    loop(1, 4, lambda k: q_copy(k).start())
    pending.append(lambda: loop(1, 4, lambda k: q_copy(k).wait_send()))
    qb[xh, c] = qsend[c]
    num[...] = jnp.zeros_like(num)
    half4 = iota((512, 128), 1) < 64

    def attend(part, which):
        block = kvb[part, which].reshape(512, 128)
        weight = jnp.exp2(dot_t(qb[...].reshape(512, 128), block)).astype(BF)
        num[...] += dot(weight, jnp.where(half4, 1.0, block.astype(F32)).astype(BF))

    def pass_on(part):
        for k in (1, 3, 2, 0):
            if k > 0:
                kv_wait(part, 2 * k)
            kv_wait(part, 2 * k + 1)
            forward(part, k).start()
            pending.append(forward(part, k).wait_send)

    pass_on(0)
    pass_on(1)
    loop(1, 4, lambda k: q_copy(k).wait_recv())
    attend(0, core)
    attend(1, core)
    for k in range(4):
        forward(0, k).wait_recv()
    attend(0, 1 - core)
    for k in range(4):
        forward(1, k).wait_recv()
    attend(1, 1 - core)
    result = num[...].astype(BF)
    for hi in range(2):
        for cc in range(2):
            for zz in range(8):
                start = ((hi * 2 + cc) * 8 + zz) * 16
                ob[hi, zz, 16 * cc : 16 * cc + 16] = result[start : start + 16]

    owner_c = lax.div(z, 4)

    def r_copy(k):
        to_z = lax.rem(z + k // 2, 8)
        to_xh = lax.rem(xh + k % 2, 2)
        slot = 2 * lax.rem(z, 4) + c
        return remote(
            ob.at[to_xh, ORDER.index((8 - k // 2) % 8)],
            rb.at[slot, xh],
            r_send.at[k],
            r_recv.at[2 * slot + xh],
            dev(to_z, y, 2 * to_xh + owner_c, core),
        )

    mine = owner_c == c

    @pl.when(jnp.logical_not(mine))
    def _():
        r_copy(0).start()

    for k in (8, 9, 7, 11, 6, 10, 5, 13, 4, 12, 3, 15, 2, 14, 1):
        r_copy(k).start()

    @pl.when(mine)
    def _():
        rb[2 * lax.rem(z, 4) + c, xh] = ob[xh, 0]

    own_slot = jnp.where(mine, 2 * (2 * lax.rem(z, 4) + c) + xh, -1)

    def r_wait(s):
        @pl.when(s != own_slot)
        def _():
            remote(
                ob.at[0, 0],
                rb.at[lax.div(s, 2), lax.rem(s, 2)],
                r_send.at[0],
                r_recv.at[s],
                partner,
            ).wait_recv()


    def finish_returns():
        @pl.when(jnp.logical_not(mine))
        def _():
            r_copy(0).wait_send()

        for k in range(1, 16):
            r_copy(k).wait_send()

    pending.append(finish_returns)
    for wait in pending:
        wait()
    loop(0, 16, r_wait)
    half3 = iota((32, 128), 1) < 64
    for p in range(4):
        even = rb[2 * p, 0].astype(F32) + rb[2 * p, 1].astype(F32)
        odd = rb[2 * p + 1, 0].astype(F32) + rb[2 * p + 1, 1].astype(F32)
        upper = jnp.where(half3, pltpu.roll(even, 64, 1), odd)
        lower = jnp.where(half3, even, pltpu.roll(odd, 64, 1))
        coarse_out[0, :, 128 * p : 128 * p + 128] = (upper / lower).astype(BF)


def shards(
    image,
    timestep,
    class_label,
    class_table,
    fine_modulation,
    coarse_modulation,
    fine_project,
    fine_output,
    fine_scales,
    merge_weight,
    coarse_project,
    coarse_scales,
):
    hbm = pl.BlockSpec(memory_space=pl.ANY)
    vmem = pltpu.VMEM
    smem = pltpu.SMEM
    dma = pltpu.SemaphoreType.DMA
    return pl.pallas_call(
        kernel,
        out_shape=(
            pltpu.VMEM((4, 128, 256), BF),
            pltpu.VMEM((1, 32, 512), BF),
        ),
        in_specs=[hbm] * 12,
        out_specs=(pl.BlockSpec(memory_space=vmem),) * 2,
        scratch_shapes=[
            vmem((10, 128, 512), BF),
            vmem((1000, 256), BF),
            vmem((256, 512), BF),
            vmem((256, 512), BF),
            vmem((512, 768), BF),
            vmem((512, 768), BF),
            vmem((2, 2, 128, 512), BF),
            vmem((4, 2048, 512), BF),
            vmem((24, 512), BF),
            vmem((4, 4, 128, 256), BF),
            vmem((10, 128, 256), BF),
            vmem((10, 128, 256), BF),
            vmem((4, 128, 256), BF),
            vmem((4, 128, 256), BF),
            vmem((2, 16, 512), BF),
            vmem((8, 2, 16, 512), BF),
            vmem((2, 8, 512), F32),
            vmem((2, 4, 4, 32, 512), BF),
            vmem((2, 2, 256, 512), BF),
            vmem((2, 2, 64, 128), BF),
            vmem((2, 128, 128), BF),
            vmem((2, 2, 4, 2, 64, 128), BF),
            vmem((2, 2, 128, 128), BF),
            vmem((512, 128), F32),
            vmem((2, 8, 32, 128), BF),
            vmem((8, 2, 32, 128), BF),
            smem((1,), jnp.int32),
            smem((1,), jnp.int32),
            smem((8,), F32),
            smem((16,), F32),
            pltpu.SemaphoreType.REGULAR((3,)),
            dma((14,)),
            dma((4,)),
            dma((6,)),
            dma((6,)),
            dma((3,)),
            dma((3,)),
            dma((4,)),
            dma((4,)),
            dma((4,)),
            dma((8,)),
            dma((8,)),
            dma((16,)),
            dma((16,)),
            dma((16,)),
            dma((16,)),
            dma((4,)),
            dma((4,)),
            dma((8,)),
            dma((8,)),
            dma((16,)),
            dma((16,)),
        ],
        compiler_params=pltpu.CompilerParams(
            collective_id=0, has_side_effects=True, vmem_limit_bytes=56 * 1024 * 1024
        ),
    )(
        timestep,
        class_label,
        fine_scales,
        coarse_scales,
        image,
        class_table,
        fine_modulation,
        coarse_modulation,
        fine_project,
        fine_output.reshape(2, 128, 512),
        merge_weight.reshape(4, 2048, 512),
        coarse_project.T,
    )


def solution(mesh):
    in_specs = (
        P("band", None, None),
        P(),
        P(),
        P(),
        P(),
        P(None, "col"),
        P(None, "col"),
        P("col", None),
        P(),
        P(None, "col"),
        P("col", "band"),
        P(),
    )
    out_specs = (P("band", None, "col"), P("band", None, "col"))
    return jax.shard_map(shards, mesh=mesh, in_specs=in_specs, out_specs=out_specs, check_vma=False)
```
